128 devices in a mesh: slab: 32 (over y_hi, x, z), dp: 4 (over y_lo, core).
Axes of the slice: x: 4, y: 4 (y_hi: 2, y_lo: 2; y = y_hi * 2 + y_lo), z: 4, core: 2. Of those that a mesh axis runs over, the one named last changes fastest.
Arguments:
- coarse_in: bfloat16 [4, 2, 64, 4, 8, 256], P('dp', None, 'slab'), may hold values from -6 to 6
- pre_up: bfloat16 [4, 2, 128, 8, 16, 128], P('dp', None, 'slab'), may hold values from -6 to 6
- pre_mid: bfloat16 [4, 2, 128, 8, 16, 128], P('dp', None, 'slab'), may hold values from -6 to 6
- grad_out: bfloat16 [4, 2, 128, 8, 16, 128], P('dp', None, 'slab'), may hold values from -6 to 6
- master: float32 [13824, 128], P(('slab', 'dp')), may hold values from -0.109375 to 0.109375
- moment: float32 [13824, 128], P(('slab', 'dp')), may hold values from -18 to 18
- second: float32 [13824, 128], P(('slab', 'dp')), may hold values from 1 to 30
Outputs:
- coarse_grad: bfloat16 [4, 2, 64, 4, 8, 256], P('dp', None, 'slab')
- new_master: float32 [13824, 128], P(('slab', 'dp'))
- new_moment: float32 [13824, 128], P(('slab', 'dp'))
- new_second: float32 [13824, 128], P(('slab', 'dp'))
The draws below stay inside these ranges and needn't reach their ends.
All inputs are finite; a program needn't handle non-finite values.
Results may differ from the reference program's by a relative error of at most 0.0075.
Values may be sent and summed in bfloat16 or wider, within the bound.
A program may use at most 128 MiB of HBM per device.

```python
import math
import jax
import jax.numpy as jnp
from jax import lax

C = 128
C2 = 256
SPG = 2
H = 8
W = 16
GROUPS = 4
SAMPLES = 8
FD = 128
CD = 64
CH = 4
CW = 8
PROWS = 13824


def block_levels(stream_key, dims, pieces, least, high):
    factor_of, own = 1.0, jax.random.fold_in(stream_key, 6)
    for position, parts in pieces:
        steps = jnp.exp(jax.random.uniform(jax.random.fold_in(own, position), (parts,), jnp.float32, least / len(pieces), high / len(pieces)))
        factor_of = factor_of * jnp.repeat(steps, dims[position] // parts).reshape([-1 if axis == position else 1 for axis in range(len(dims))])
    return factor_of


def noise(own_key, dims, deviation, reach, cuts=(), held_as=jnp.bfloat16):
    array = jax.random.normal(own_key, dims, jnp.float32) * deviation
    if len(cuts) > 0:
        array = block_levels(own_key, dims, cuts, -0.22, 0.18) * array
    return jnp.clip(array, min=-reach, max=reach).astype(held_as)


def setup_inputs(seed: int = 0) -> dict:
    key_of = jax.random.split(jax.random.key(seed), 8)
    coarse_in = noise(key_of[0], (GROUPS, SPG, CD, CH, CW, C2), 1.0, 6.0, ((0, 4), (2, 32)))
    pre_up = noise(key_of[1], (GROUPS, SPG, FD, H, W, C), 1.0, 6.0, ((0, 4), (2, 32)))
    pre_mid = noise(key_of[2], (GROUPS, SPG, FD, H, W, C), 1.0, 6.0, ((0, 4), (2, 32)))
    grad_out = noise(key_of[3], (GROUPS, SPG, FD, H, W, C), 1.0, 6.0, ((0, 4), (2, 32)))
    master = noise(key_of[4], (PROWS, C), (27 * C) ** -0.5, 0.109375, ((0, 128),), jnp.float32)
    moment = noise(key_of[5], (PROWS, C), 3.0, 18.0, ((0, 128),), jnp.float32)
    second = jnp.clip(jnp.exp(math.log(30.0) - 3.4011974 * jax.random.uniform(key_of[6], (PROWS, C), jnp.float32) ** block_levels(key_of[6], (PROWS, C), ((0, 128),), -0.2, 0.2)), 1.0, 30.0)
    return dict(coarse_in=coarse_in, pre_up=pre_up, pre_mid=pre_mid, grad_out=grad_out, master=master, moment=moment, second=second)


beta_one = 0.9
beta_two = 0.999
adam_step = 10.0
learn_rate = 0.01
adam_eps = 1e-08

def correlate(padded, weight):
    samples_here, depth_ext, height, breadth, in_width = padded.shape
    inner_depth = depth_ext - 2
    lateral = jnp.pad(padded, ((0, 0), (0, 0), (1, 1), (1, 1), (0, 0)))
    running = None
    for depth_tap in range(3):
        for row_tap in range(3):
            columns = jnp.concatenate([lateral[:, depth_tap:depth_tap + inner_depth, row_tap:row_tap + height, col_tap:col_tap + breadth, :] for col_tap in range(3)], axis=-1)
            row_start = (depth_tap * 3 + row_tap) * 3 * in_width
            product_term = jnp.dot(columns.reshape(-1, 3 * in_width), weight[row_start:row_start + 3 * in_width], preferred_element_type=jnp.float32)
            running = product_term if running is None else running + product_term
    return running.reshape(samples_here, inner_depth, height, breadth, weight.shape[1])

def filter_grad(padded, grads):
    samples_here, depth_ext, height, breadth, in_width = padded.shape
    inner_depth = depth_ext - 2
    lateral = jnp.pad(padded, ((0, 0), (0, 0), (1, 1), (1, 1), (0, 0)))
    flat_grads = grads.reshape(-1, grads.shape[-1])
    blocks = []
    for depth_tap in range(3):
        for row_tap in range(3):
            columns = jnp.concatenate([lateral[:, depth_tap:depth_tap + inner_depth, row_tap:row_tap + height, col_tap:col_tap + breadth, :] for col_tap in range(3)], axis=-1)
            blocks.append(lax.dot_general(columns.reshape(-1, 3 * in_width), flat_grads, (((0,), (0,)), ((), ())), preferred_element_type=jnp.float32))
    return jnp.concatenate(blocks, axis=0)

def flipped(weight, in_width):
    out_width = weight.shape[1]
    shaped = weight.reshape(3, 3, 3, in_width, out_width)[::-1, ::-1, ::-1]
    return shaped.transpose(0, 1, 2, 4, 3).reshape(27 * out_width, in_width)

def upconv_back(grad_pad, coarse, weight):
    lateral = jnp.pad(grad_pad, ((0, 0), (0, 0), (1, 0), (1, 0), (0, 0)))
    samples_here, coarse_depth, coarse_rows, coarse_cols, coarse_width = coarse.shape
    fine_width = weight.shape[1]
    slices = []
    for depth_tap in range(3):
        for row_tap in range(3):
            for col_tap in range(3):
                slices.append(lateral[:, depth_tap:depth_tap + 2 * coarse_depth:2, row_tap:row_tap + 2 * coarse_rows:2, col_tap:col_tap + 2 * coarse_cols:2, :])
    gathered = jnp.concatenate(slices, axis=-1).reshape(-1, 27 * fine_width)
    turned = weight.reshape(27, coarse_width, fine_width).transpose(0, 2, 1).reshape(27 * fine_width, coarse_width)
    coarse_grad = jnp.dot(gathered, turned, preferred_element_type=jnp.float32).reshape(coarse.shape)
    filter_part = lax.dot_general(coarse.reshape(-1, coarse_width), gathered, (((0,), (0,)), ((), ())), preferred_element_type=jnp.float32)
    filter_part = filter_part.reshape(coarse_width, 27, fine_width).transpose(1, 0, 2).reshape(27 * coarse_width, fine_width)
    return (coarse_grad, filter_part)

def pad_depth(values):
    return jnp.pad(values, ((0, 0), (1, 1), (0, 0), (0, 0), (0, 0)))

def reference(coarse_in, pre_up, pre_mid, grad_out, master, moment, second):
    channels = pre_up.shape[-1]
    weights = master.astype(jnp.bfloat16)
    w_one = weights[:27 * channels]
    w_two = weights[27 * channels:54 * channels]
    w_up = weights[54 * channels:]
    flip_one = flipped(w_one, channels)
    flip_two = flipped(w_two, channels)
    coarse_all = coarse_in.reshape((-1,) + coarse_in.shape[2:])
    up_all = pre_up.reshape((-1,) + pre_up.shape[2:])
    mid_all = pre_mid.reshape((-1,) + pre_mid.shape[2:])
    out_all = grad_out.reshape((-1,) + grad_out.shape[2:])

    def one_sample(carried, inputs):
        coarse = inputs[0][None]
        up_in = inputs[1][None]
        mid_in = inputs[2][None]
        out_in = inputs[3][None]
        mid_act = jax.nn.relu(pad_depth(mid_in))
        grad_two = filter_grad(mid_act, out_in)
        back_mid = correlate(pad_depth(out_in), flip_two)
        mid_grad = jnp.where(mid_in > 0, back_mid, 0.0).astype(jnp.bfloat16)
        up_act = jax.nn.relu(pad_depth(up_in))
        grad_one = filter_grad(up_act, mid_grad)
        back_up = correlate(pad_depth(mid_grad), flip_one)
        up_grad = jnp.where(up_in > 0, back_up, 0.0).astype(jnp.bfloat16)
        grad_pad = jnp.pad(up_grad, ((0, 0), (1, 0), (0, 0), (0, 0), (0, 0)))
        coarse_grad, grad_up = upconv_back(grad_pad, coarse, w_up)
        carried = carried + jnp.concatenate([grad_one, grad_two, grad_up], axis=0)
        return (carried, coarse_grad[0].astype(jnp.bfloat16))
    initial = jnp.zeros(master.shape, jnp.float32)
    totals, coarse_grads = lax.scan(one_sample, initial, (coarse_all, up_all, mid_all, out_all))
    mean_grad = totals / SAMPLES
    new_moment = beta_one * moment + (1.0 - beta_one) * mean_grad
    new_second = beta_two * second + (1.0 - beta_two) * mean_grad * mean_grad
    corrected = new_moment / (1.0 - beta_one ** adam_step)
    scaled = jnp.sqrt(new_second / (1.0 - beta_two ** adam_step)) + adam_eps
    new_master = master - learn_rate * corrected / scaled
    return (coarse_grads.reshape(coarse_in.shape), new_master, new_moment, new_second)
```

```python
import jax
import jax.numpy as jnp
from jax import lax
from jax.experimental import pallas as pl
from jax.experimental.pallas import tpu as pltpu
from jax.sharding import PartitionSpec as P

beta_one = 0.9
beta_two = 0.999
adam_step = 10.0
learn_rate = 0.01
adam_eps = 1e-08

F32 = jnp.float32
BF16 = jnp.bfloat16
MESH = pl.DeviceIdType.MESH

ROWS = 108
TOTAL = 13824
FILTER = 3456
START = (0, 48, 80)
HOLD = (48, 32, 32)
VALID = (48, 32, 28)
ORDER = (("y", "z", "x"), ("z", "x", "y"), ("x", "y", "z"))


def nt(left, right):
    return lax.dot_general(
        left, right, (((1,), (1,)), ((), ())), preferred_element_type=F32
    )


def nn(left, right):
    return jnp.dot(left, right, preferred_element_type=F32)


def kernel(
    master, grad_out, pre_mid, pre_up, coarse,
    coarse_grad, summed,
    g0, g1, g2, sb0, sb1, sb2, rb0, rb1, rb2, t0, t1, t2, ra0, ra1, ra2,
    u0, u1, u2, rc0, rc1, rc2, v0, v1, v2, rd0, rd1, rd2,
    wflat, fflat, w_one, w_two, w_up, x_out, x_mid, act_t, mid_raw, up_raw, gathered, halo_out, halo_mid,
    ag_send, ag_recv, core_send, core_recv, rs_send, rs_recv, swap_send, swap_recv,
    halo_send, halo_recv,
):
    gat, sbs, rbs, tot = (g0, g1, g2), (sb0, sb1, sb2), (rb0, rb1, rb2), (t0, t1, t2)
    ras, us, rcs, vs, rds = (
        (ra0, ra1, ra2), (u0, u1, u2), (rc0, rc1, rc2), (v0, v1, v2), (rd0, rd1, rd2),
    )
    slab, dp = lax.axis_index("slab"), lax.axis_index("dp")
    at = {
        "x": lax.rem(slab // 4, 4),
        "y": (slab // 16) * 2 + dp // 2,
        "z": lax.rem(slab, 4),
    }
    core = lax.rem(dp, 2)
    other = 1 - core

    def device(where, which):
        return (
            (where["y"] // 2) * 16 + where["x"] * 4 + where["z"],
            lax.rem(where["y"], 2) * 2 + which,
        )

    def ahead(axis, step):
        moved = dict(at)
        moved[axis] = lax.rem(at[axis] + step, 4)
        return device(moved, core)

    def back(axis, step):
        return lax.rem(at[axis] + 4 - step, 4)

    partner = device(at, other)
    after = (lax.rem(slab + 1, 32), dp)
    before = (lax.rem(slab + 31, 32), dp)

    def copy(src, dst, send, recv, target):
        return pltpu.make_async_remote_copy(
            src_ref=src, dst_ref=dst, send_sem=send, recv_sem=recv,
            device_id=target, device_id_type=MESH,
        )

    barrier = pltpu.get_barrier_semaphore()
    targets = [partner, after, before]
    targets += [ahead(axis, step) for axis in ("x", "y", "z") for step in (1, 2, 3)]
    for target in targets:
        pl.semaphore_signal(barrier, inc=1, device_id=target, device_id_type=MESH)

    for part in range(3):
        axes = ORDER[part]
        rows = master[START[part] : START[part] + VALID[part], :]
        if HOLD[part] > VALID[part]:
            rows = jnp.concatenate(
                [rows, jnp.zeros((HOLD[part] - VALID[part], 128), F32)], axis=0
            )
        gat[part][core, at[axes[2]], at[axes[1]], at[axes[0]]] = rows.astype(BF16)
    pl.semaphore_wait(barrier, len(targets))

    started = []

    def go(c):
        c.start()
        started.append(c)
        return c

    halo_up = go(copy(grad_out.at[:, 3], halo_out.at[0], halo_send.at[0], halo_recv.at[0], after))
    halo_down = go(copy(grad_out.at[:, 0], halo_out.at[1], halo_send.at[1], halo_recv.at[1], before))

    def piece(part, which, level, coords):
        axes = ORDER[part]
        place = [coords[axes[2]], coords[axes[1]], coords[axes[0]]][: 3 - level]
        return gat[part].at[tuple([which] + place)]

    def gather_copy(part, level, step):
        src = piece(part, core, level, at)
        sem = (part, level, step - 1)
        return copy(src, src, ag_send.at[sem], ag_recv.at[sem], ahead(ORDER[part][level], step))

    def arrived(part, level, step, which):
        moved = dict(at)
        moved[ORDER[part][level]] = back(ORDER[part][level], step)
        return piece(part, which, level, moved)

    def gather_start(level):
        for step in (1, 3, 2):
            for part in range(3):
                go(gather_copy(part, level, step))

    def core_copy(part, number, ref):
        return copy(ref, ref, core_send.at[part, number], core_recv.at[part, number], partner)

    def gather_wait(level, passed):
        for step in (1, 3, 2):
            for part in range(3):
                ref = arrived(part, level, step, core)
                sem = (part, level, step - 1)
                copy(ref, ref, ag_send.at[sem], ag_recv.at[sem], partner).wait_recv()
                if passed:
                    go(core_copy(part, (level - 1) * 3 + step, ref))

    gather_start(0)

    row = lax.broadcasted_iota(jnp.int32, (128, 128), 0)
    lane = lax.broadcasted_iota(jnp.int32, (128, 128), 1)
    breadth = lax.rem(row, 16)
    for ext in (x_out, x_mid):
        ext[:, :, 0] = jnp.zeros((2, 6, 16, 384), BF16)
        ext[:, :, 9] = jnp.zeros((2, 6, 16, 384), BF16)
    fflat[TOTAL : TOTAL + 8, :] = jnp.zeros((8, 128), F32)

    def widen(ext, sample, layer, value):
        later = jnp.where(breadth == 15, 0.0, pltpu.roll(value, 127, 0))
        earlier = jnp.where(breadth == 0, 0.0, pltpu.roll(value, 1, 0))
        wide = jnp.concatenate(
            [later.astype(BF16), value.astype(BF16), earlier.astype(BF16)], axis=1
        )
        ext[sample, layer, 1:9] = wide.reshape(8, 16, 384)

    def transposed_act(pre):
        for sample in range(2):
            for layer in range(4):
                value = jnp.maximum(pre[sample, layer].reshape(128, 128).astype(F32), 0.0)
                turned = value.T
                first = sample * 4 + layer
                columns = slice(first * 128, first * 128 + 128)
                low = jnp.where(lane < 16, 0.0, pltpu.roll(turned, 16, 1))
                high = jnp.where(lane >= 112, 0.0, pltpu.roll(turned, 112, 1))
                act_t[0:128, columns] = low.astype(BF16)
                act_t[128:256, columns] = turned.astype(BF16)
                act_t[256:384, columns] = high.astype(BF16)

    def own_layers(index, carry):
        sample, layer = index // 4, lax.rem(index, 4)
        widen(x_out, sample, layer + 1, grad_out[sample, layer].reshape(128, 128).astype(F32))
        return carry

    def edges(ext, halo):
        for sample in range(2):
            low = halo[0, sample].reshape(128, 128).astype(F32)
            widen(ext, sample, 0, jnp.where(slab > 0, low, 0.0))
            high = halo[1, sample].reshape(128, 128).astype(F32)
            widen(ext, sample, 5, jnp.where(slab < 31, high, 0.0))

    def filter_grad(ext, first, depth):
        right = ext[:, 2 - depth : 6 - depth, 1:9].reshape(1024, 384)
        out = nn(act_t[...], right)
        for height in range(3):
            for col in range(3):
                start = first + ((depth * 3 + height) * 3 + col) * 128
                fflat[start : start + 128, :] = out[
                    height * 128 : height * 128 + 128, col * 128 : col * 128 + 128
                ]

    def back_conv(ext, weight, layer):
        acc = jnp.zeros((256, 128), F32)
        for depth in range(3):
            for height in range(3):
                left = ext[:, layer + 2 - depth, 2 - height : 10 - height].reshape(256, 384)
                acc = acc + nt(left, weight[depth * 3 + height])
        return acc

    transposed_act(pre_mid)
    lax.fori_loop(0, 8, own_layers, 0)
    gather_wait(0, False)
    gather_start(1)
    for part in range(3):
        go(core_copy(part, 0, piece(part, core, 1, at)))
    halo_up.wait_recv()
    halo_down.wait_recv()
    edges(x_out, halo_out)
    filter_grad(x_out, FILTER, 1)
    gather_wait(1, True)
    gather_start(2)
    filter_grad(x_out, FILTER, 0)
    filter_grad(x_out, FILTER, 2)
    gather_wait(2, True)
    for part in range(3):
        for number in range(7):
            if number == 0:
                ref = piece(part, other, 1, at)
            else:
                ref = arrived(part, 1 + (number - 1) // 3, (number - 1) % 3 + 1, other)
            core_copy(part, number, ref).wait_recv()

    def place(chip, which):
        where = {"x": lax.rem(chip // 8, 4), "y": (chip // 32) * 2 + lax.rem(chip, 2), "z": lax.rem(chip // 2, 4)}
        return where

    def unpack(chip, carry):
        where = place(chip, 0)
        base = pl.multiple_of(chip * 216, 8)
        pieces = []
        for which in range(2):
            for part in range(3):
                axes = ORDER[part]
                value = gat[part][which, where[axes[2]], where[axes[1]], where[axes[0]]]
                pieces.append(value.astype(F32)[: VALID[part]])
        wflat[pl.ds(base, 216), :] = jnp.concatenate(pieces, axis=0)
        return carry

    lax.fori_loop(0, 64, unpack, 0)

    def taps(index, carry):
        for col in range(3):
            columns = slice(col * 128, col * 128 + 128)
            start = pl.multiple_of((index * 3 + col) * 128, 128)
            w_one[index, :, columns] = wflat[pl.ds(start, 128), :].astype(BF16)
            w_two[index, :, columns] = wflat[pl.ds(start + FILTER, 128), :].astype(BF16)
            start = pl.multiple_of((index * 3 + col) * 256, 128)
            w_up[index, :, columns] = wflat[pl.ds(start + 2 * FILTER, 256), :].astype(BF16)
        return carry

    lax.fori_loop(0, 9, taps, 0)

    def mid_layer(index, carry):
        layer = lax.rem(index + 3, 4)
        value = back_conv(x_out, w_two, layer)
        keep = pre_mid[:, layer].reshape(256, 128).astype(F32) > 0.0
        value = jnp.where(keep, value, 0.0).astype(BF16)
        mid_raw[:, layer] = value.reshape(2, 8, 16, 128)
        for sample in range(2):
            widen(x_mid, sample, layer + 1, value[sample * 128 : sample * 128 + 128].astype(F32))
        return carry

    lax.fori_loop(0, 2, mid_layer, 0)
    mid_up = go(copy(mid_raw.at[:, 3], halo_mid.at[0], halo_send.at[2], halo_recv.at[2], after))
    mid_down = go(copy(mid_raw.at[:, 0], halo_mid.at[1], halo_send.at[3], halo_recv.at[3], before))
    lax.fori_loop(2, 4, mid_layer, 0)
    transposed_act(pre_up)
    filter_grad(x_mid, 0, 1)
    mid_up.wait_recv()
    mid_down.wait_recv()
    edges(x_mid, halo_mid)

    def up_layer(index, carry):
        layer = lax.rem(index + 3, 4)
        value = back_conv(x_mid, w_one, layer)
        keep = pre_up[:, layer].reshape(256, 128).astype(F32) > 0.0
        value = jnp.where(keep, value, 0.0).astype(BF16)
        up_raw[:, layer + 1] = value.reshape(2, 128, 128)
        return carry

    lax.fori_loop(0, 1, up_layer, 0)
    up_next = go(copy(up_raw.at[:, 4], up_raw.at[:, 0], halo_send.at[4], halo_recv.at[4], after))
    lax.fori_loop(1, 4, up_layer, 0)
    filter_grad(x_mid, 0, 0)
    filter_grad(x_mid, 0, 2)
    up_next.wait_recv()

    pick_row = lax.broadcasted_iota(jnp.int32, (288, 128), 0)
    pick_lane = lax.broadcasted_iota(jnp.int32, (288, 128), 1)
    tap, coarse_row, coarse_col = pick_row // 32, lax.rem(pick_row // 8, 4), lax.rem(pick_row, 8)
    fine_row = 2 * coarse_row + tap // 3 - 1
    fine_col = 2 * coarse_col + lax.rem(tap, 3) - 1
    chosen = (fine_row >= 0) & (fine_col >= 0) & (pick_lane == fine_row * 16 + fine_col)
    pick = jnp.where(chosen, 1.0, 0.0).astype(BF16)
    for sample in range(2):
        for layer in range(5):
            value = up_raw[sample, layer]
            if layer == 0:
                value = jnp.where(slab > 0, value.astype(F32), 0.0).astype(BF16)
            picked = nn(pick, value).astype(BF16)
            for depth, quarter in ((layer, 0), (layer - 2, 1)):
                if 0 <= depth < 3:
                    first = (sample * 2 + quarter) * 32
                    for tap in range(9):
                        column = (depth * 9 + tap) * 128
                        gathered[first : first + 32, column : column + 128] = picked[
                            tap * 32 : tap * 32 + 32
                        ]
    acc = jnp.zeros((128, 256), F32)
    coarse_t = coarse[...].reshape(128, 256).astype(F32).T.astype(BF16)
    for index in range(9):
        column = index * 384
        block = gathered[:, column : column + 384]
        acc = acc + nt(block, w_up[index])
        out = nn(coarse_t, block)
        for col in range(3):
            start = 2 * FILTER + (index * 3 + col) * 256
            fflat[start : start + 256, :] = out[:, col * 128 : col * 128 + 128]
    coarse_grad[...] = acc.astype(BF16)

    def pack(chip, carry):
        where = place(chip, 0)
        base = pl.multiple_of(chip * 216, 8)
        value = fflat[pl.ds(base, 224), :]
        for which in range(2):
            for part in range(3):
                axes = ORDER[part]
                start = which * ROWS + START[part]
                rows = value[start : start + HOLD[part]].astype(BF16)
                sbs[part][which, where[axes[2]], where[axes[1]], where[axes[0]]] = rows
        return carry

    lax.fori_loop(0, 64, pack, 0)
    swaps = [
        go(copy(sbs[part].at[other], rbs[part], swap_send.at[part], swap_recv.at[part], partner))
        for part in range(3)
    ]

    def scatter(part, level, src, dst):
        axis = ORDER[part][2 - level]
        out = []
        for step in (1, 3, 2):
            sem = (part, level, step - 1)
            out.append(
                go(
                    copy(
                        src.at[lax.rem(at[axis] + step, 4)], dst.at[step - 1],
                        rs_send.at[sem], rs_recv.at[sem], ahead(axis, step),
                    )
                )
            )
        return out

    first = []
    for part in range(3):
        swaps[part].wait_recv()

        def add(index, carry, part=part):
            total = sbs[part][core, index // 4, lax.rem(index, 4)].astype(F32)
            total = total + rbs[part][index // 4, lax.rem(index, 4)].astype(F32)
            tot[part][index // 4, lax.rem(index, 4)] = total.astype(BF16)
            return carry

        lax.fori_loop(0, 16, add, 0)
        first.append(scatter(part, 0, tot[part], ras[part]))
    second = []
    for part in range(3):
        for c in first[part]:
            c.wait_recv()
        mine = at[ORDER[part][2]]

        def add(index, carry, part=part, mine=mine):
            total = tot[part][mine, index].astype(F32)
            for step in range(3):
                total = total + ras[part][step, index].astype(F32)
            us[part][index] = total.astype(BF16)
            return carry

        lax.fori_loop(0, 4, add, 0)
        second.append(scatter(part, 1, us[part], rcs[part]))
    third = []
    for part in range(3):
        for c in second[part]:
            c.wait_recv()
        total = us[part][at[ORDER[part][1]]].astype(F32)
        for step in range(3):
            total = total + rcs[part][step].astype(F32)
        vs[part][...] = total.astype(BF16)
        third.append(scatter(part, 2, vs[part], rds[part]))
    for part in range(3):
        for c in third[part]:
            c.wait_recv()
        total = vs[part][at[ORDER[part][0]]].astype(F32)
        for step in range(3):
            total = total + rds[part][step].astype(F32)
        summed[START[part] : START[part] + VALID[part], :] = total[: VALID[part]]
    for c in started:
        c.wait_send()


def body(coarse_in, pre_up, pre_mid, grad_out, master, moment, second):
    vmem = pl.BlockSpec(memory_space=pltpu.VMEM)
    scratch = []
    for shape in ((2, 4, 4, 4), (2, 4, 4, 4), (4, 4, 4), (4, 4, 4), (3, 4, 4), (4, 4), (3, 4), (4,), (3,)):
        scratch += [pltpu.VMEM(shape + (hold, 128), BF16) for hold in HOLD]
    scratch += [
        pltpu.VMEM((TOTAL, 128), F32),
        pltpu.VMEM((TOTAL + 8, 128), F32),
        pltpu.VMEM((9, 128, 384), BF16),
        pltpu.VMEM((9, 128, 384), BF16),
        pltpu.VMEM((9, 256, 384), BF16),
        pltpu.VMEM((2, 6, 10, 16, 384), BF16),
        pltpu.VMEM((2, 6, 10, 16, 384), BF16),
        pltpu.VMEM((384, 1024), BF16),
        pltpu.VMEM((2, 4, 8, 16, 128), BF16),
        pltpu.VMEM((2, 5, 128, 128), BF16),
        pltpu.VMEM((128, FILTER), BF16),
        pltpu.VMEM((2, 2, 8, 16, 128), BF16),
        pltpu.VMEM((2, 2, 8, 16, 128), BF16),
    ]
    for shape in ((3, 3, 3), (3, 7), (3, 3, 3), (3,), (5,)):
        scratch += [pltpu.SemaphoreType.DMA(shape)] * 2
    coarse_grad, summed = pl.pallas_call(
        kernel,
        out_shape=(
            jax.ShapeDtypeStruct((128, 256), BF16),
            jax.ShapeDtypeStruct((ROWS, 128), F32),
        ),
        in_specs=[vmem] * 5,
        out_specs=(vmem, vmem),
        scratch_shapes=scratch,
        compiler_params=pltpu.CompilerParams(
            collective_id=0, has_side_effects=True, vmem_limit_bytes=56 * 1024 * 1024
        ),
    )(
        master,
        grad_out.reshape(grad_out.shape[1:]),
        pre_mid.reshape(pre_mid.shape[1:]),
        pre_up.reshape(pre_up.shape[1:]),
        coarse_in.reshape(128, 256),
    )
    mean_grad = summed / 8.0
    new_moment = beta_one * moment + (1.0 - beta_one) * mean_grad
    new_second = beta_two * second + (1.0 - beta_two) * mean_grad * mean_grad
    corrected = new_moment / (1.0 - beta_one**adam_step)
    scaled = jnp.sqrt(new_second / (1.0 - beta_two**adam_step)) + adam_eps
    new_master = master - learn_rate * corrected / scaled
    return (coarse_grad.reshape(coarse_in.shape), new_master, new_moment, new_second)


def solution(mesh):
    wide = P("dp", None, "slab", None, None, None)
    flat = P(("slab", "dp"), None)
    return jax.shard_map(
        body,
        mesh=mesh,
        in_specs=(wide, wide, wide, wide, flat, flat, flat),
        out_specs=(wide, flat, flat, flat),
        check_vma=False,
    )
```

```python
import jax
import jax.numpy as jnp
from jax import lax
from jax.experimental import pallas as pl
from jax.experimental.pallas import tpu as pltpu
from jax.sharding import PartitionSpec as P

beta_one = 0.9
beta_two = 0.999
adam_step = 10.0
learn_rate = 0.01
adam_eps = 1e-08

F32 = jnp.float32
BF16 = jnp.bfloat16
MESH = pl.DeviceIdType.MESH

ROWS = 108
TOTAL = 13824
FILTER = 3456
START = (0, 48, 80)
HOLD = (48, 32, 32)
VALID = (48, 32, 28)
ORDER = (("y", "z", "x"), ("y", "x", "z"), ("z", "x", "y"))
EARLY, LATE = 0, 1


def nt(left, right):
    return lax.dot_general(
        left, right, (((1,), (1,)), ((), ())), preferred_element_type=F32
    )


def nn(left, right):
    return jnp.dot(left, right, preferred_element_type=F32)


def kernel(
    master, grad_out, pre_mid, pre_up, coarse,
    coarse_grad, summed,
    g0, g1, g2, sb0, sb1, sb2, rb0, rb1, rb2, t0, t1, t2, ra0, ra1, ra2,
    u0, u1, u2, rc0, rc1, rc2, v0, v1, v2, rd0, rd1, rd2,
    wflat, fflat, w_one, w_two, w_up, x_out, x_mid, act_t, mid_raw, up_raw, gathered, halo_out, halo_mid,
    ag_send, ag_recv, core_send, core_recv, rs_send, rs_recv, swap_send, swap_recv,
    halo_send, halo_recv,
):
    gat, sbs, rbs, tot = (g0, g1, g2), (sb0, sb1, sb2), (rb0, rb1, rb2), (t0, t1, t2)
    ras, us, rcs, vs, rds = (
        (ra0, ra1, ra2), (u0, u1, u2), (rc0, rc1, rc2), (v0, v1, v2), (rd0, rd1, rd2),
    )
    slab, dp = lax.axis_index("slab"), lax.axis_index("dp")
    at = {
        "x": lax.rem(slab // 4, 4),
        "y": (slab // 16) * 2 + dp // 2,
        "z": lax.rem(slab, 4),
    }
    core = lax.rem(dp, 2)
    other = 1 - core

    def device(where, which):
        return (
            (where["y"] // 2) * 16 + where["x"] * 4 + where["z"],
            lax.rem(where["y"], 2) * 2 + which,
        )

    def moved(axis, step):
        where = dict(at)
        where[axis] = lax.rem(at[axis] + step, 4)
        return where

    def ahead(axis, step):
        return device(moved(axis, step), core)

    partner = device(at, other)
    after = (lax.rem(slab + 1, 32), dp)
    before = (lax.rem(slab + 31, 32), dp)

    def copy(src, dst, send, recv, target):
        return pltpu.make_async_remote_copy(
            src_ref=src, dst_ref=dst, send_sem=send, recv_sem=recv,
            device_id=target, device_id_type=MESH,
        )

    barrier = pltpu.get_barrier_semaphore()
    targets = [partner, after, before]
    targets += [ahead(axis, step) for axis in ("x", "y", "z") for step in (1, 2, 3)]
    for target in targets:
        pl.semaphore_signal(barrier, inc=1, device_id=target, device_id_type=MESH)

    def block(ref, part, lead, where):
        axes = ORDER[part]
        if part == 2:
            inner = [lax.rem(where["y"], 2), where["x"], where["z"]]
        else:
            inner = [where[axes[2]], where[axes[1]], lax.rem(where["y"], 2)]
        return tuple([where["y"] // 2] + lead + inner)

    for part in range(3):
        rows = master[START[part] : START[part] + VALID[part], :]
        if HOLD[part] > VALID[part]:
            rows = jnp.concatenate(
                [rows, jnp.zeros((HOLD[part] - VALID[part], 128), F32)], axis=0
            )
        gat[part][block(gat[part], part, [core], at)] = rows.astype(BF16)
    pl.semaphore_wait(barrier, len(targets))

    started = []

    def go(c):
        c.start()
        started.append(c)
        return c

    def piece(part, which, level, half, where):
        place = block(gat[part], part, [which], where)
        if part == 2:
            return gat[part].at[place[: 5 - level]]
        if level == 0:
            return gat[part].at[place]
        return gat[part].at[(half,) + place[1 : 5 - level]]

    def gather(part, level, half):
        axis = ORDER[part][level]
        out = []
        for step in (1, 3, 2):
            sem = (part, level, step - 1, half)
            src = piece(part, core, level, half, at)
            go(copy(src, src, ag_send.at[sem], ag_recv.at[sem], ahead(axis, step)))
            dst = piece(part, core, level, half, moved(axis, 4 - step))
            out.append(copy(dst, dst, ag_send.at[sem], ag_recv.at[sem], partner))
        return out

    def core_copy(part, half, number, which):
        axis = ORDER[part][2]
        ref = piece(part, which, 2, half, moved(axis, 4 - number))
        sem = (part, half, number)
        return copy(ref, ref, core_send.at[sem], core_recv.at[sem], partner)

    def wait_for(copies):
        for c in copies:
            c.wait_recv()

    leg = [gather(part, 0, EARLY) for part in range(3)]
    halo_up = go(copy(grad_out.at[:, 3], halo_out.at[0], halo_send.at[0], halo_recv.at[0], after))
    halo_down = go(copy(grad_out.at[:, 0], halo_out.at[1], halo_send.at[1], halo_recv.at[1], before))

    row = lax.broadcasted_iota(jnp.int32, (128, 128), 0)
    lane = lax.broadcasted_iota(jnp.int32, (128, 128), 1)
    breadth = lax.rem(row, 16)
    for ext in (x_out, x_mid):
        ext[:, :, 0] = jnp.zeros((2, 6, 16, 384), BF16)
        ext[:, :, 9] = jnp.zeros((2, 6, 16, 384), BF16)
    fflat[TOTAL : TOTAL + 8, :] = jnp.zeros((8, 128), F32)

    def widen(ext, sample, layer, value):
        later = jnp.where(breadth == 15, 0.0, pltpu.roll(value, 127, 0))
        earlier = jnp.where(breadth == 0, 0.0, pltpu.roll(value, 1, 0))
        wide = jnp.concatenate(
            [later.astype(BF16), value.astype(BF16), earlier.astype(BF16)], axis=1
        )
        ext[sample, layer, 1:9] = wide.reshape(8, 16, 384)

    def transposed_act(pre):
        for sample in range(2):
            for layer in range(4):
                value = jnp.maximum(pre[sample, layer].reshape(128, 128).astype(F32), 0.0)
                turned = value.T
                first = sample * 4 + layer
                columns = slice(first * 128, first * 128 + 128)
                low = jnp.where(lane < 16, 0.0, pltpu.roll(turned, 16, 1))
                high = jnp.where(lane >= 112, 0.0, pltpu.roll(turned, 112, 1))
                act_t[0:128, columns] = low.astype(BF16)
                act_t[128:256, columns] = turned.astype(BF16)
                act_t[256:384, columns] = high.astype(BF16)

    def own_layers(index, carry):
        sample, layer = index // 4, lax.rem(index, 4)
        widen(x_out, sample, layer + 1, grad_out[sample, layer].reshape(128, 128).astype(F32))
        return carry

    def edges(ext, halo):
        for sample in range(2):
            low = halo[0, sample].reshape(128, 128).astype(F32)
            widen(ext, sample, 0, jnp.where(slab > 0, low, 0.0))
            high = halo[1, sample].reshape(128, 128).astype(F32)
            widen(ext, sample, 5, jnp.where(slab < 31, high, 0.0))

    def filter_grad(ext, first, depth):
        right = ext[:, 2 - depth : 6 - depth, 1:9].reshape(1024, 384)
        out = nn(act_t[...], right)
        for height in range(3):
            for col in range(3):
                start = first + ((depth * 3 + height) * 3 + col) * 128
                fflat[start : start + 128, :] = out[
                    height * 128 : height * 128 + 128, col * 128 : col * 128 + 128
                ]

    def back_conv(ext, weight, layer):
        acc = jnp.zeros((256, 128), F32)
        for depth in range(3):
            for height in range(3):
                left = ext[:, layer + 2 - depth, 2 - height : 10 - height].reshape(256, 384)
                acc = acc + nt(left, weight[depth * 3 + height])
        return acc

    def place(chip):
        return {"x": lax.rem(chip // 8, 4), "y": (chip // 32) * 2 + lax.rem(chip, 2), "z": lax.rem(chip // 2, 4)}

    def unpack(chip, carry):
        where = place(chip)
        base = pl.multiple_of(chip * 216, 8)
        pieces = []
        for which in range(2):
            for part in range(3):
                value = gat[part][block(gat[part], part, [which], where)]
                pieces.append(value.astype(F32)[: VALID[part]])
        wflat[pl.ds(base, 216), :] = jnp.concatenate(pieces, axis=0)
        return carry

    def taps(weight, first, width):
        def one(index, carry):
            for col in range(3):
                start = pl.multiple_of((index * 3 + col) * width + first, 128)
                weight[index, :, col * 128 : col * 128 + 128] = wflat[pl.ds(start, width), :].astype(BF16)
            return carry

        lax.fori_loop(0, 9, one, 0)

    def pack(chip, carry):
        where = place(chip)
        base = pl.multiple_of(chip * 216, 8)
        value = fflat[pl.ds(base, 224), :]
        for which in range(2):
            for part in range(3):
                start = which * ROWS + START[part]
                rows = value[start : start + HOLD[part]].astype(BF16)
                sbs[part][block(sbs[part], part, [which], where)] = rows
        return carry

    transposed_act(pre_mid)
    for part in range(3):
        wait_for(leg[part])
    leg = [gather(part, 1, EARLY) for part in range(3)]
    later_leg = [gather(part, 1, LATE) for part in range(2)]
    lax.fori_loop(0, 8, own_layers, 0)
    filter_grad(x_out, FILTER, 1)
    third = []
    for part in range(3):
        wait_for(leg[part])
        third.append(gather(part, 2, EARLY))
        go(core_copy(part, EARLY, 0, core))
    halo_up.wait_recv()
    halo_down.wait_recv()
    edges(x_out, halo_out)
    filter_grad(x_out, FILTER, 0)
    filter_grad(x_out, FILTER, 2)
    lax.fori_loop(16, 32, pack, 0)

    def forward(part, half, copies):
        for step, c in zip((1, 3, 2), copies):
            c.wait_recv()
            go(core_copy(part, half, step, core))

    for part in range(3):
        forward(part, EARLY, third[part])
    late_third = []
    for part in range(2):
        wait_for(later_leg[part])
        late_third.append(gather(part, 2, LATE))
        go(core_copy(part, LATE, 0, core))
    for part in range(3):
        wait_for([core_copy(part, EARLY, number, other) for number in range(4)])

    lax.fori_loop(16, 32, unpack, 0)
    taps(w_two, FILTER, 128)

    def mid_layer(index, carry):
        layer = lax.rem(index + 3, 4)
        value = back_conv(x_out, w_two, layer)
        keep = pre_mid[:, layer].reshape(256, 128).astype(F32) > 0.0
        value = jnp.where(keep, value, 0.0).astype(BF16)
        mid_raw[:, layer] = value.reshape(2, 8, 16, 128)
        for sample in range(2):
            widen(x_mid, sample, layer + 1, value[sample * 128 : sample * 128 + 128].astype(F32))
        return carry

    lax.fori_loop(0, 2, mid_layer, 0)
    mid_up = go(copy(mid_raw.at[:, 3], halo_mid.at[0], halo_send.at[2], halo_recv.at[2], after))
    mid_down = go(copy(mid_raw.at[:, 0], halo_mid.at[1], halo_send.at[3], halo_recv.at[3], before))
    lax.fori_loop(2, 4, mid_layer, 0)
    lax.fori_loop(0, 16, unpack, 0)
    taps(w_one, 0, 128)
    transposed_act(pre_up)
    filter_grad(x_mid, 0, 1)
    for part in range(2):
        forward(part, LATE, late_third[part])
    mid_up.wait_recv()
    mid_down.wait_recv()
    edges(x_mid, halo_mid)

    def up_layer(index, carry):
        layer = lax.rem(index + 3, 4)
        value = back_conv(x_mid, w_one, layer)
        keep = pre_up[:, layer].reshape(256, 128).astype(F32) > 0.0
        value = jnp.where(keep, value, 0.0).astype(BF16)
        up_raw[:, layer + 1] = value.reshape(2, 128, 128)
        return carry

    lax.fori_loop(0, 1, up_layer, 0)
    up_next = go(copy(up_raw.at[:, 4], up_raw.at[:, 0], halo_send.at[4], halo_recv.at[4], after))
    filter_grad(x_mid, 0, 0)
    filter_grad(x_mid, 0, 2)
    lax.fori_loop(0, 16, pack, 0)

    def swap(half):
        return [
            go(
                copy(
                    sbs[part].at[half, other], rbs[part].at[half],
                    swap_send.at[part, half], swap_recv.at[part, half], partner,
                )
            )
            for part in range(3)
        ]

    def scatter(part, level, src, dst, sems):
        axis = ORDER[part][2 - level]
        out = []
        for step in (1, 3, 2):
            sem = (part, level, step - 1, sems)
            out.append(
                go(
                    copy(
                        src.at[lax.rem(at[axis] + step, 4)], dst.at[step - 1],
                        rs_send.at[sem], rs_recv.at[sem], ahead(axis, step),
                    )
                )
            )
        return out

    def core_sum(part, half, swapped):
        swapped[part].wait_recv()
        outer, inner = (2, 4) if part == 2 else (4, 4)

        def add(index, carry):
            a, b = index // inner, lax.rem(index, inner)
            total = sbs[part][half, core, a, b].astype(F32) + rbs[part][half, a, b].astype(F32)
            tot[part][half, a, b] = total.astype(BF16)
            return carry

        lax.fori_loop(0, outer * inner, add, 0)

    column = []
    for step in (1, 3, 2):
        where = moved("y", step)
        sem = (2, 0, step - 1, 0)
        c = copy(
            tot[2].at[where["y"] // 2, lax.rem(where["y"], 2)], ras[2].at[step - 1],
            rs_send.at[sem], rs_recv.at[sem], device(where, core),
        )
        column.append((where["y"] // 2, c))

    def first_sums(half, swapped):
        out = []
        core_sum(2, half, swapped)
        for owner, c in column:
            pl.when(owner == half)(c.start)
        for part in range(2):
            core_sum(part, half, swapped)
            out.append(scatter(part, 0, tot[part].at[half], ras[part].at[half], half))
        return out

    def second_sums(part, half, copies):
        wait_for(copies)
        mine = at[ORDER[part][2]]

        def add(index, carry):
            total = tot[part][half, mine, index].astype(F32)
            for step in range(3):
                total = total + ras[part][half, step, index].astype(F32)
            us[part][half, index] = total.astype(BF16)
            return carry

        lax.fori_loop(0, 4, add, 0)
        return scatter(part, 1, us[part].at[half], rcs[part].at[half], half)

    def third_sums(part, half, copies):
        wait_for(copies)
        total = us[part][half, at[ORDER[part][1]]].astype(F32)
        for step in range(3):
            total = total + rcs[part][half, step].astype(F32)
        vs[part][2 * half : 2 * half + 2] = total.astype(BF16)

    early_swap = swap(EARLY)
    lax.fori_loop(1, 4, up_layer, 0)
    early_first = first_sums(EARLY, early_swap)
    up_next.wait_recv()

    pick_row = lax.broadcasted_iota(jnp.int32, (288, 128), 0)
    pick_lane = lax.broadcasted_iota(jnp.int32, (288, 128), 1)
    tap, coarse_row, coarse_col = pick_row // 32, lax.rem(pick_row // 8, 4), lax.rem(pick_row, 8)
    fine_row = 2 * coarse_row + tap // 3 - 1
    fine_col = 2 * coarse_col + lax.rem(tap, 3) - 1
    chosen = (fine_row >= 0) & (fine_col >= 0) & (pick_lane == fine_row * 16 + fine_col)
    pick = jnp.where(chosen, 1.0, 0.0).astype(BF16)
    for sample in range(2):
        for layer in range(5):
            value = up_raw[sample, layer]
            if layer == 0:
                value = jnp.where(slab > 0, value.astype(F32), 0.0).astype(BF16)
            picked = nn(pick, value).astype(BF16)
            for depth, quarter in ((layer, 0), (layer - 2, 1)):
                if 0 <= depth < 3:
                    first = (sample * 2 + quarter) * 32
                    for tap in range(9):
                        columns = slice((depth * 9 + tap) * 128, (depth * 9 + tap) * 128 + 128)
                        gathered[first : first + 32, columns] = picked[tap * 32 : tap * 32 + 32]
    coarse_t = coarse[...].reshape(128, 256).astype(F32).T.astype(BF16)
    for index in range(9):
        out = nn(coarse_t, gathered[:, index * 384 : index * 384 + 384])
        for col in range(3):
            start = 2 * FILTER + (index * 3 + col) * 256
            fflat[start : start + 256, :] = out[:, col * 128 : col * 128 + 128]
    lax.fori_loop(32, 64, pack, 0)
    late_swap = swap(LATE)
    for part in range(2):
        wait_for([core_copy(part, LATE, number, other) for number in range(4)])
    late_first = first_sums(LATE, late_swap)

    early_second = [second_sums(part, EARLY, early_first[part]) for part in range(2)]
    lax.fori_loop(32, 64, unpack, 0)
    taps(w_up, 2 * FILTER, 256)
    acc = jnp.zeros((128, 256), F32)
    for index in range(9):
        acc = acc + nt(gathered[:, index * 384 : index * 384 + 384], w_up[index])
    coarse_grad[...] = acc.astype(BF16)
    for part in range(2):
        third_sums(part, EARLY, early_second[part])

    for _, c in column:
        c.wait_recv()
    mine = (at["y"] // 2, lax.rem(at["y"], 2))

    def add_plane(index, carry):
        total = tot[2][mine[0], mine[1], index].astype(F32)
        for step in range(3):
            total = total + ras[2][step, index].astype(F32)
        us[2][index] = total.astype(BF16)
        return carry

    lax.fori_loop(0, 4, add_plane, 0)
    plane = scatter(2, 1, us[2], rcs[2], 0)
    late_second = [second_sums(part, LATE, late_first[part]) for part in range(2)]
    wait_for(plane)
    total = us[2][at["x"]].astype(F32)
    for step in range(3):
        total = total + rcs[2][step].astype(F32)
    vs[2][...] = total.astype(BF16)
    last = [None, None, scatter(2, 2, vs[2], rds[2], 0)]
    for part in range(2):
        third_sums(part, LATE, late_second[part])
        last[part] = scatter(part, 2, vs[part], rds[part], 0)
    for part in (2, 0, 1):
        wait_for(last[part])
        total = vs[part][at[ORDER[part][0]]].astype(F32)
        for step in range(3):
            total = total + rds[part][step].astype(F32)
        summed[START[part] : START[part] + VALID[part], :] = total[: VALID[part]]
    for c in started:
        c.wait_send()
    for _, c in column:
        c.wait_send()


def body(coarse_in, pre_up, pre_mid, grad_out, master, moment, second):
    vmem = pl.BlockSpec(memory_space=pltpu.VMEM)
    scratch = []
    for shape, column in (
        ((2, 2, 4, 4, 2), (2, 2, 2, 4, 4)),
        ((2, 2, 4, 4, 2), (2, 2, 2, 4, 4)),
        ((2, 4, 4, 2), (2, 2, 4, 4)),
        ((2, 4, 4, 2), (2, 2, 4, 4)),
        ((2, 3, 4, 2), (3, 4, 4)),
        ((2, 4, 2), (4, 4)),
        ((2, 3, 2), (3, 4)),
        ((4,), (4,)),
        ((3,), (3,)),
    ):
        for part in range(3):
            lead = column if part == 2 else shape
            scratch.append(pltpu.VMEM(lead + (HOLD[part], 128), BF16))
    scratch += [
        pltpu.VMEM((TOTAL, 128), F32),
        pltpu.VMEM((TOTAL + 8, 128), F32),
        pltpu.VMEM((9, 128, 384), BF16),
        pltpu.VMEM((9, 128, 384), BF16),
        pltpu.VMEM((9, 256, 384), BF16),
        pltpu.VMEM((2, 6, 10, 16, 384), BF16),
        pltpu.VMEM((2, 6, 10, 16, 384), BF16),
        pltpu.VMEM((384, 1024), BF16),
        pltpu.VMEM((2, 4, 8, 16, 128), BF16),
        pltpu.VMEM((2, 5, 128, 128), BF16),
        pltpu.VMEM((128, FILTER), BF16),
        pltpu.VMEM((2, 2, 8, 16, 128), BF16),
        pltpu.VMEM((2, 2, 8, 16, 128), BF16),
    ]
    for shape in ((3, 3, 3, 2), (3, 2, 4), (3, 3, 3, 2), (3, 2), (5,)):
        scratch += [pltpu.SemaphoreType.DMA(shape)] * 2
    coarse_grad, summed = pl.pallas_call(
        kernel,
        out_shape=(
            jax.ShapeDtypeStruct((128, 256), BF16),
            jax.ShapeDtypeStruct((ROWS, 128), F32),
        ),
        in_specs=[vmem] * 5,
        out_specs=(vmem, vmem),
        scratch_shapes=scratch,
        compiler_params=pltpu.CompilerParams(
            collective_id=0, has_side_effects=True, vmem_limit_bytes=56 * 1024 * 1024
        ),
    )(
        master,
        grad_out.reshape(grad_out.shape[1:]),
        pre_mid.reshape(pre_mid.shape[1:]),
        pre_up.reshape(pre_up.shape[1:]),
        coarse_in.reshape(128, 256),
    )
    mean_grad = summed / 8.0
    new_moment = beta_one * moment + (1.0 - beta_one) * mean_grad
    new_second = beta_two * second + (1.0 - beta_two) * mean_grad * mean_grad
    corrected = new_moment / (1.0 - beta_one**adam_step)
    scaled = jnp.sqrt(new_second / (1.0 - beta_two**adam_step)) + adam_eps
    new_master = master - learn_rate * corrected / scaled
    return (coarse_grad.reshape(coarse_in.shape), new_master, new_moment, new_second)


def solution(mesh):
    wide = P("dp", None, "slab", None, None, None)
    flat = P(("slab", "dp"), None)
    return jax.shard_map(
        body,
        mesh=mesh,
        in_specs=(wide, wide, wide, wide, flat, flat, flat),
        out_specs=(wide, flat, flat, flat),
        check_vma=False,
    )
```

```python
import jax
import jax.numpy as jnp
from jax import lax
from jax.experimental import pallas as pl
from jax.experimental.pallas import tpu as pltpu
from jax.sharding import PartitionSpec as P

beta_one = 0.9
beta_two = 0.999
adam_step = 10.0
learn_rate = 0.01
adam_eps = 1e-08

F32 = jnp.float32
BF16 = jnp.bfloat16
MESH = pl.DeviceIdType.MESH

ROWS = 108
TOTAL = 13824
FILTER = 3456
START = (0, 48, 80)
HOLD = (48, 32, 32)
VALID = (48, 32, 28)
ORDER = (("y", "z", "x"), ("y", "x", "z"), ("z", "x", "y"))
EARLY, LATE = 0, 1


def nt(left, right):
    return lax.dot_general(
        left, right, (((1,), (1,)), ((), ())), preferred_element_type=F32
    )


def nn(left, right):
    return jnp.dot(left, right, preferred_element_type=F32)


def kernel(
    master_in, grad_out_in, pre_mid_in, pre_up_in, coarse_in,
    coarse_grad, summed,
    master, grad_out, pre_mid, pre_up, coarse,
    g0, g1, g2, sb0, sb1, sb2, rb0, rb1, rb2, t0, t1, t2, ra0, ra1, ra2,
    u0, u1, u2, rc0, rc1, rc2, v0, v1, v2, rd0, rd1, rd2,
    wflat, fflat, w_one, w_two, w_up, x_out, x_mid, act_mid, act_up, mid_raw, up_raw, up_before,
    gathered, lowest, halo_out, halo_mid, halo_up,
    ag_send, ag_recv, core_send, core_recv, rs_send, rs_recv, swap_send, swap_recv,
    halo_send, halo_recv, load_sem, token_sem,
):
    gat, sbs, rbs, tot = (g0, g1, g2), (sb0, sb1, sb2), (rb0, rb1, rb2), (t0, t1, t2)
    ras, us, rcs, vs, rds = (
        (ra0, ra1, ra2), (u0, u1, u2), (rc0, rc1, rc2), (v0, v1, v2), (rd0, rd1, rd2),
    )
    slab, dp = lax.axis_index("slab"), lax.axis_index("dp")
    at = {
        "x": lax.rem(slab // 4, 4),
        "y": (slab // 16) * 2 + dp // 2,
        "z": lax.rem(slab, 4),
    }
    core = lax.rem(dp, 2)
    other = 1 - core

    def device(where, which):
        return (
            (where["y"] // 2) * 16 + where["x"] * 4 + where["z"],
            lax.rem(where["y"], 2) * 2 + which,
        )

    def moved(axis, step):
        where = dict(at)
        where[axis] = lax.rem(at[axis] + step, 4)
        return where

    def ahead(axis, step):
        return device(moved(axis, step), core)

    partner = device(at, other)
    after = (lax.rem(slab + 1, 32), dp)
    before = (lax.rem(slab + 31, 32), dp)

    def copy(src, dst, send, recv, target):
        return pltpu.make_async_remote_copy(
            src_ref=src, dst_ref=dst, send_sem=send, recv_sem=recv,
            device_id=target, device_id_type=MESH,
        )

    barrier = pltpu.get_barrier_semaphore()
    targets = [partner]
    targets += [ahead(axis, step) for axis in ("x", "y", "z") for step in (1, 2, 3)]
    for target in targets:
        pl.semaphore_signal(barrier, inc=1, device_id=target, device_id_type=MESH)

    def block(ref, part, lead, where):
        axes = ORDER[part]
        if part == 2:
            inner = [lax.rem(where["y"], 2), where["x"], where["z"]]
        else:
            inner = [where[axes[2]], where[axes[1]], lax.rem(where["y"], 2)]
        return tuple([where["y"] // 2] + lead + inner)

    loads = [
        pltpu.make_async_copy(src, dst, load_sem.at[number])
        for number, (src, dst) in enumerate(
            (
                (master_in, master),
                (grad_out_in, grad_out),
                (pre_mid_in, pre_mid),
                (pre_up_in, pre_up),
                (coarse_in, coarse.at[0, :, 0:2]),
            )
        )
    ]
    for load in loads:
        load.start()

    loads[0].wait()
    for part in range(3):
        rows = master[START[part] : START[part] + VALID[part], :]
        if HOLD[part] > VALID[part]:
            rows = jnp.concatenate(
                [rows, jnp.zeros((HOLD[part] - VALID[part], 128), F32)], axis=0
            )
        gat[part][block(gat[part], part, [core], at)] = rows.astype(BF16)
    pl.semaphore_wait(barrier, len(targets))

    started = []

    def go(c):
        c.start()
        started.append(c)
        return c

    def piece(part, which, level, half, where):
        place = block(gat[part], part, [which], where)
        if part == 2:
            return gat[part].at[place[: 5 - level]]
        if level == 0:
            return gat[part].at[place]
        return gat[part].at[(half,) + place[1 : 5 - level]]

    def back_half(step):
        return lax.rem(at["y"] + 4 - step, 4) // 2

    def gather(part, level, half):
        axis = ORDER[part][level]
        out = []
        for step in (1, 3, 2):
            sem = (part, level, step - 1, half)
            src = piece(part, core, level, half, at)
            go(copy(src, src, ag_send.at[sem], ag_recv.at[sem], ahead(axis, step)))
            dst = piece(part, core, level, half, moved(axis, 4 - step))
            out.append(copy(dst, dst, ag_send.at[sem], ag_recv.at[sem], partner))
        return out

    tall_half = at["y"] // 2
    tall = []
    for step in (1, 3, 2):
        sem = (2, 2, step - 1, 0)
        src = piece(2, core, 2, 0, at)
        dst = piece(2, core, 2, 0, moved("y", 4 - step))
        tall.append(
            (
                step,
                back_half(step),
                copy(src, src, ag_send.at[sem], ag_recv.at[sem], ahead("y", step)),
                copy(dst, dst, ag_send.at[sem], ag_recv.at[sem], partner),
            )
        )

    def tall_start(half):
        for _, _, c, _ in tall:
            pl.when(tall_half == half)(c.start)

    def tall_forward(half):
        for step, owner, _, c in tall:

            @pl.when(owner == half)
            def _():
                c.wait_recv()
                core_copy(2, 0, step, core).start()

    def tall_partner(half):
        for step, owner, _, _ in tall:
            pl.when(owner == half)(core_copy(2, 0, step, other).wait_recv)

    def core_copy(part, half, number, which):
        axis = ORDER[part][2]
        ref = piece(part, which, 2, half, moved(axis, 4 - number))
        sem = (part, half, number)
        return copy(ref, ref, core_send.at[sem], core_recv.at[sem], partner)

    def wait_for(copies):
        for c in copies:
            c.wait_recv()

    leg = [gather(part, 0, EARLY) for part in range(3)]
    for step in (1, 3, 2):
        pl.semaphore_signal(token_sem.at[0], inc=1, device_id=ahead("z", step), device_id_type=MESH)

    row = lax.broadcasted_iota(jnp.int32, (128, 128), 0)
    lane = lax.broadcasted_iota(jnp.int32, (128, 128), 1)
    breadth = lax.rem(row, 16)
    for ext in (x_out, x_mid):
        ext[:, :, 0] = jnp.zeros((2, 6, 16, 384), BF16)
        ext[:, :, 9] = jnp.zeros((2, 6, 16, 384), BF16)
    fflat[TOTAL : TOTAL + 8, :] = jnp.zeros((8, 128), F32)

    def widen(ext, sample, layer, value):
        later = jnp.where(breadth == 15, 0.0, pltpu.roll(value, 127, 0))
        earlier = jnp.where(breadth == 0, 0.0, pltpu.roll(value, 1, 0))
        wide = jnp.concatenate(
            [later.astype(BF16), value.astype(BF16), earlier.astype(BF16)], axis=1
        )
        ext[sample, layer, 1:9] = wide.reshape(8, 16, 384)

    def turn(act_t, first, value):
        turned = jnp.maximum(value, 0.0).T
        columns = slice(first * 128, first * 128 + 128)
        low = jnp.where(lane < 16, 0.0, pltpu.roll(turned, 16, 1))
        high = jnp.where(lane >= 112, 0.0, pltpu.roll(turned, 112, 1))
        act_t[0:128, columns] = low.astype(BF16)
        act_t[128:256, columns] = turned.astype(BF16)
        act_t[256:384, columns] = high.astype(BF16)

    def transposed_act(act_t, pre, depth, first):
        for sample in range(2):
            for layer in range(4):
                value = pre[sample, layer].reshape(128, 128).astype(F32)
                turn(act_t, sample * depth + first + layer, value)

    def transposed_edges(act_t, halo):
        for sample in range(2):
            low = halo[0, sample].reshape(128, 128).astype(F32)
            turn(act_t, sample * 6, jnp.where(slab > 0, low, 0.0))
            high = halo[1, sample].reshape(128, 128).astype(F32)
            turn(act_t, sample * 6 + 5, jnp.where(slab < 31, high, 0.0))

    def own_layers(index, carry):
        sample, layer = index // 4, lax.rem(index, 4)
        widen(x_out, sample, layer + 1, grad_out[sample, layer].reshape(128, 128).astype(F32))
        return carry

    def edges(ext, halo):
        for sample in range(2):
            low = halo[0, sample].reshape(128, 128).astype(F32)
            widen(ext, sample, 0, jnp.where(slab > 0, low, 0.0))
            high = halo[1, sample].reshape(128, 128).astype(F32)
            widen(ext, sample, 5, jnp.where(slab < 31, high, 0.0))

    def grad_by_cotangent(ext, act_t, first, depth):
        right = ext[:, 2 - depth : 6 - depth, 1:9].reshape(1024, 384)
        store_grad(first, depth, nn(act_t[...], right))

    def grad_by_act(ext, act_t, first, depth):
        out = jnp.zeros((384, 384), F32)
        for sample in range(2):
            start = (sample * 6 + depth) * 128
            out = out + nn(act_t[:, start : start + 512], ext[sample, 1:5, 1:9].reshape(512, 384))
        store_grad(first, depth, out)

    def store_grad(first, depth, out):
        for height in range(3):
            for col in range(3):
                start = first + ((depth * 3 + height) * 3 + col) * 128
                fflat[start : start + 128, :] = out[
                    height * 128 : height * 128 + 128, col * 128 : col * 128 + 128
                ]

    def back_conv(ext, weight, layer):
        acc = jnp.zeros((256, 128), F32)
        for depth in range(3):
            for height in range(3):
                left = ext[:, layer + 2 - depth, 2 - height : 10 - height].reshape(256, 384)
                acc = acc + nt(left, weight[depth * 3 + height])
        return acc

    def place(chip):
        return {"x": lax.rem(chip // 8, 4), "y": (chip // 32) * 2 + lax.rem(chip, 2), "z": lax.rem(chip // 2, 4)}

    def unpack(chip, carry):
        where = place(chip)
        base = pl.multiple_of(chip * 216, 8)
        pieces = []
        for which in range(2):
            for part in range(3):
                value = gat[part][block(gat[part], part, [which], where)]
                pieces.append(value.astype(F32)[: VALID[part]])
        wflat[pl.ds(base, 216), :] = jnp.concatenate(pieces, axis=0)
        return carry

    def taps(weight, first, width):
        def one(index, carry):
            for col in range(3):
                start = pl.multiple_of((index * 3 + col) * width + first, 128)
                weight[index, :, col * 128 : col * 128 + 128] = wflat[pl.ds(start, width), :].astype(BF16)
            return carry

        lax.fori_loop(0, 9, one, 0)

    def pack(chip, carry):
        where = place(chip)
        base = pl.multiple_of(chip * 216, 8)
        value = fflat[pl.ds(base, 224), :]
        for which in range(2):
            for part in range(3):
                start = which * ROWS + START[part]
                rows = value[start : start + HOLD[part]].astype(BF16)
                sbs[part][block(sbs[part], part, [which], where)] = rows
        return carry

    def pack_late(chip, carry):
        where = place(chip)
        base = pl.multiple_of(chip * 216, 8)
        value = fflat[pl.ds(base, 224), :]
        value = jnp.where(core == 0, value[0:112], value[ROWS : ROWS + 112])
        for part in range(3):
            rows = value[START[part] : START[part] + HOLD[part]].astype(BF16)
            tot[part][block(tot[part], part, [], where)] = rows
        return carry

    for load in loads[1:]:
        load.wait()
    transposed_act(act_mid, pre_mid, 4, 0)
    for part in range(3):
        wait_for(leg[part])
    leg = [gather(part, 1, EARLY) for part in range(3)]
    pl.semaphore_wait(token_sem.at[0], 3)
    pl.semaphore_signal(token_sem.at[1], inc=1, device_id=ahead("y", 2), device_id_type=MESH)
    lax.fori_loop(0, 8, own_layers, 0)
    grad_by_cotangent(x_out, act_mid, FILTER, 1)
    pl.semaphore_wait(token_sem.at[1], 1)
    halos = []
    for number, (src, dst, target) in enumerate(
        (
            (grad_out.at[:, 3], halo_out.at[0], after),
            (grad_out.at[:, 0], halo_out.at[1], before),
            (pre_up.at[:, 3], halo_up.at[0], after),
            (pre_up.at[:, 0], halo_up.at[1], before),
            (coarse.at[0, :, 0], coarse.at[0, :, 2], before),
        )
    ):
        sem = 3 + number
        halos.append(go(copy(src, dst, halo_send.at[sem], halo_recv.at[sem], target)))
    third = []
    for part in (2, 0, 1):
        wait_for(leg[part])
        if part == 2:
            tall_start(EARLY)
        else:
            third.append(gather(part, 2, EARLY))
        go(core_copy(part, EARLY, 0, core))
    leg = [gather(part, 1, LATE) for part in range(2)]
    transposed_act(act_up, pre_up, 6, 1)
    wait_for(halos[0:2])
    edges(x_out, halo_out)
    grad_by_cotangent(x_out, act_mid, FILTER, 0)
    grad_by_cotangent(x_out, act_mid, FILTER, 2)
    lax.fori_loop(16, 32, pack, 0)

    def forward(part, half, copies):
        for step, c in zip((1, 3, 2), copies):
            c.wait_recv()
            go(core_copy(part, half, step, core))

    tall_forward(EARLY)
    for part in range(2):
        forward(part, EARLY, third[part])
    third = []
    for part in range(2):
        wait_for(leg[part])
        third.append(gather(part, 2, LATE))
        go(core_copy(part, LATE, 0, core))
    tall_start(LATE)
    core_copy(2, EARLY, 0, other).wait_recv()
    tall_partner(EARLY)
    for part in range(2):
        wait_for([core_copy(part, EARLY, number, other) for number in range(4)])

    def swap(half):
        return [
            go(
                copy(
                    sbs[part].at[half, other], rbs[part].at[half],
                    swap_send.at[part, half], swap_recv.at[part, half], partner,
                )
            )
            for part in range(3)
        ]

    lax.fori_loop(16, 32, unpack, 0)
    taps(w_two, FILTER, 128)

    def mid_layer(index, carry):
        layer = lax.rem(index + 3, 4)
        value = back_conv(x_out, w_two, layer)
        keep = pre_mid[:, layer].reshape(256, 128).astype(F32) > 0.0
        value = jnp.where(keep, value, 0.0).astype(BF16)
        mid_raw[:, layer] = value.reshape(2, 8, 16, 128)
        for sample in range(2):
            widen(x_mid, sample, layer + 1, value[sample * 128 : sample * 128 + 128].astype(F32))
        return carry

    lax.fori_loop(0, 2, mid_layer, 0)
    mid_up = go(copy(mid_raw.at[:, 3], halo_mid.at[0], halo_send.at[0], halo_recv.at[0], after))
    mid_down = go(copy(mid_raw.at[:, 0], halo_mid.at[1], halo_send.at[1], halo_recv.at[1], before))
    lax.fori_loop(2, 4, mid_layer, 0)
    lax.fori_loop(0, 16, unpack, 0)
    taps(w_one, 0, 128)
    wait_for(halos[2:])
    pair = go(copy(coarse.at[0], coarse.at[1], halo_send.at[8], halo_recv.at[8], partner))
    transposed_edges(act_up, halo_up)
    for depth in range(3):
        grad_by_act(x_mid, act_up, 0, depth)
    lax.fori_loop(0, 16, pack, 0)
    early_swap = swap(EARLY)
    tall_forward(LATE)
    for part in range(2):
        forward(part, LATE, third[part])
    mid_up.wait_recv()
    mid_down.wait_recv()
    edges(x_mid, halo_mid)

    def up_layer(index, carry):
        layer = lax.rem(index + 3, 4)
        value = back_conv(x_mid, w_one, layer)
        keep = pre_up[:, layer].reshape(256, 128).astype(F32) > 0.0
        value = jnp.where(keep, value, 0.0).astype(BF16)
        up_raw[0, :, layer] = value.reshape(2, 128, 128)
        return carry

    lax.fori_loop(0, 4, up_layer, 0)
    up_pair = go(copy(up_raw.at[0], up_raw.at[1], halo_send.at[2], halo_recv.at[2], partner))
    up_next = go(copy(up_raw.at[0, :, 3], up_before, halo_send.at[9], halo_recv.at[9], after))

    def scatter(part, level, src, dst, sems):
        axis = ORDER[part][2 - level]
        out = []
        for step in (1, 3, 2):
            sem = (part, level, step - 1, sems)
            out.append(
                go(
                    copy(
                        src.at[lax.rem(at[axis] + step, 4)], dst.at[step - 1],
                        rs_send.at[sem], rs_recv.at[sem], ahead(axis, step),
                    )
                )
            )
        return out

    def core_sum(part, half, swapped):
        swapped[part].wait_recv()
        outer, inner = (2, 4) if part == 2 else (4, 4)

        def add(index, carry):
            a, b = index // inner, lax.rem(index, inner)
            total = sbs[part][half, core, a, b].astype(F32) + rbs[part][half, a, b].astype(F32)
            tot[part][half, a, b] = total.astype(BF16)
            return carry

        lax.fori_loop(0, outer * inner, add, 0)

    column = []
    for step in (1, 3, 2):
        where = moved("y", step)
        sem = (2, 0, step - 1, 0)
        c = copy(
            tot[2].at[where["y"] // 2, lax.rem(where["y"], 2)], ras[2].at[step - 1],
            rs_send.at[sem], rs_recv.at[sem], device(where, core),
        )
        column.append((where["y"] // 2, c))

    def first_sends(half):
        for owner, c in column:
            pl.when(owner == half)(c.start)
        return [scatter(part, 0, tot[part].at[half], ras[part].at[half], half) for part in range(2)]

    def second_sums(part, half, copies):
        wait_for(copies)
        mine = at[ORDER[part][2]]

        def add(index, carry):
            total = tot[part][half, mine, index].astype(F32)
            for step in range(3):
                total = total + ras[part][half, step, index].astype(F32)
            us[part][half, index] = total.astype(BF16)
            return carry

        lax.fori_loop(0, 4, add, 0)
        return scatter(part, 1, us[part].at[half], rcs[part].at[half], half)

    def third_sums(part, half, copies):
        wait_for(copies)
        total = us[part][half, at[ORDER[part][1]]].astype(F32)
        for step in range(3):
            total = total + rcs[part][half, step].astype(F32)
        vs[part][2 * half : 2 * half + 2] = total.astype(BF16)

    for part in (2, 0, 1):
        core_sum(part, EARLY, early_swap)
    early_first = first_sends(EARLY)

    pick_row = lax.broadcasted_iota(jnp.int32, (288, 128), 0)
    pick_lane = lax.broadcasted_iota(jnp.int32, (288, 128), 1)
    tap, coarse_row, coarse_col = pick_row // 32, lax.rem(pick_row // 8, 4), lax.rem(pick_row, 8)
    fine_row = 2 * coarse_row + tap // 3 - 1
    fine_col = 2 * coarse_col + lax.rem(tap, 3) - 1
    chosen = (fine_row >= 0) & (fine_col >= 0) & (pick_lane == fine_row * 16 + fine_col)
    pick = jnp.where(chosen, 1.0, 0.0).astype(BF16)

    def spread(slot, sample, layer):
        picked = nn(pick, up_raw[slot, sample, layer]).astype(BF16)
        first = ((slot * 2 + sample) * 2 + layer // 2) * 32
        for depth in (1,) if layer % 2 == 0 else (0, 2):
            for tap in range(9):
                columns = slice((depth * 9 + tap) * 128, (depth * 9 + tap) * 128 + 128)
                gathered[first : first + 32, columns] = picked[tap * 32 : tap * 32 + 32]
        return picked

    def lower(sample, quarter, picked):
        first = (sample * 2 + quarter) * 32
        for tap in range(9):
            lowest[first : first + 32, tap * 128 : tap * 128 + 128] = picked[tap * 32 : tap * 32 + 32]

    for sample in range(2):
        for layer in range(4):
            picked = spread(0, sample, layer)
            if layer == 1:
                lower(sample, 1, picked)
    pair.wait_recv()
    turned = []
    for first in (1, 0):
        rows = []
        for slot in range(2):
            for sample in range(2):
                for quarter in (first, first + 1):
                    value = coarse[slot, sample, quarter].astype(F32)
                    if quarter == 2:
                        value = jnp.where(slab < 31, value, 0.0)
                    rows.append(value)
        turned.append(jnp.concatenate(rows, axis=0).T.astype(BF16))
    up_pair.wait_recv()
    for sample in range(2):
        for layer in range(4):
            spread(1, sample, layer)
    for index in range(9):
        out = nn(turned[min(index // 3, 1)], gathered[:, index * 384 : index * 384 + 384])
        for col in range(3):
            start = 2 * FILTER + (index * 3 + col) * 256
            fflat[start : start + 256, :] = out[:, col * 128 : col * 128 + 128]
    lax.fori_loop(32, 64, pack_late, 0)
    late_first = first_sends(LATE)

    tall_partner(LATE)
    for part in range(2):
        wait_for([core_copy(part, LATE, number, other) for number in range(4)])
    early_second = [second_sums(part, EARLY, early_first[part]) for part in range(2)]
    lax.fori_loop(32, 64, unpack, 0)
    taps(w_up, 2 * FILTER, 256)
    up_next.wait_recv()
    for sample in range(2):
        value = jnp.where(slab > 0, up_before[sample].astype(F32), 0.0).astype(BF16)
        lower(sample, 0, nn(pick, value).astype(BF16))
    acc = jnp.zeros((128, 256), F32)
    for index in range(9):
        if index < 3:
            left = lowest[:, index * 384 : index * 384 + 384]
        else:
            left = gathered[0:128, index * 384 : index * 384 + 384]
        acc = acc + nt(left, w_up[index])
    coarse_grad[...] = acc.astype(BF16)
    for part in range(2):
        third_sums(part, EARLY, early_second[part])

    for _, c in column:
        c.wait_recv()
    mine = (at["y"] // 2, lax.rem(at["y"], 2))

    def add_plane(index, carry):
        total = tot[2][mine[0], mine[1], index].astype(F32)
        for step in range(3):
            total = total + ras[2][step, index].astype(F32)
        us[2][index] = total.astype(BF16)
        return carry

    lax.fori_loop(0, 4, add_plane, 0)
    plane = scatter(2, 1, us[2], rcs[2], 0)
    late_second = [second_sums(part, LATE, late_first[part]) for part in range(2)]
    wait_for(plane)
    total = us[2][at["x"]].astype(F32)
    for step in range(3):
        total = total + rcs[2][step].astype(F32)
    vs[2][...] = total.astype(BF16)
    last = [None, None, scatter(2, 2, vs[2], rds[2], 0)]
    for part in range(2):
        third_sums(part, LATE, late_second[part])
        last[part] = scatter(part, 2, vs[part], rds[part], 0)
    for part in (2, 0, 1):
        wait_for(last[part])
        total = vs[part][at[ORDER[part][0]]].astype(F32)
        for step in range(3):
            total = total + rds[part][step].astype(F32)
        summed[START[part] : START[part] + VALID[part], :] = total[: VALID[part]]
    for c in started:
        c.wait_send()
    for _, c in column:
        c.wait_send()
    for step, _, c, _ in tall:
        c.wait_send()
        core_copy(2, 0, step, core).wait_send()


def body(coarse_in, pre_up, pre_mid, grad_out, master, moment, second):
    vmem = pl.BlockSpec(memory_space=pltpu.VMEM)
    held = pl.BlockSpec(memory_space=pl.ANY)
    scratch = [
        pltpu.VMEM((ROWS, 128), F32),
        pltpu.VMEM((2, 4, 8, 16, 128), BF16),
        pltpu.VMEM((2, 4, 8, 16, 128), BF16),
        pltpu.VMEM((2, 4, 8, 16, 128), BF16),
        pltpu.VMEM((2, 2, 3, 32, 256), BF16),
    ]
    for shape, column in (
        ((2, 2, 4, 4, 2), (2, 2, 2, 4, 4)),
        ((2, 2, 4, 4, 2), (2, 2, 2, 4, 4)),
        ((2, 4, 4, 2), (2, 2, 4, 4)),
        ((2, 4, 4, 2), (2, 2, 4, 4)),
        ((2, 3, 4, 2), (3, 4, 4)),
        ((2, 4, 2), (4, 4)),
        ((2, 3, 2), (3, 4)),
        ((4,), (4,)),
        ((3,), (3,)),
    ):
        for part in range(3):
            lead = column if part == 2 else shape
            scratch.append(pltpu.VMEM(lead + (HOLD[part], 128), BF16))
    scratch += [
        pltpu.VMEM((TOTAL, 128), F32),
        pltpu.VMEM((TOTAL + 8, 128), F32),
        pltpu.VMEM((9, 128, 384), BF16),
        pltpu.VMEM((9, 128, 384), BF16),
        pltpu.VMEM((9, 256, 384), BF16),
        pltpu.VMEM((2, 6, 10, 16, 384), BF16),
        pltpu.VMEM((2, 6, 10, 16, 384), BF16),
        pltpu.VMEM((384, 1024), BF16),
        pltpu.VMEM((384, 1536), BF16),
        pltpu.VMEM((2, 4, 8, 16, 128), BF16),
        pltpu.VMEM((2, 2, 4, 128, 128), BF16),
        pltpu.VMEM((2, 128, 128), BF16),
        pltpu.VMEM((256, FILTER), BF16),
        pltpu.VMEM((128, 9 * 128), BF16),
        pltpu.VMEM((2, 2, 8, 16, 128), BF16),
        pltpu.VMEM((2, 2, 8, 16, 128), BF16),
        pltpu.VMEM((2, 2, 8, 16, 128), BF16),
    ]
    for shape in ((3, 3, 3, 2), (3, 2, 4), (3, 3, 3, 2), (3, 2), (10,)):
        scratch += [pltpu.SemaphoreType.DMA(shape)] * 2
    scratch += [pltpu.SemaphoreType.DMA((5,)), pltpu.SemaphoreType.REGULAR((2,))]
    coarse_grad, summed = pl.pallas_call(
        kernel,
        out_shape=(
            jax.ShapeDtypeStruct((128, 256), BF16),
            jax.ShapeDtypeStruct((ROWS, 128), F32),
        ),
        in_specs=[held] * 5,
        out_specs=(vmem, vmem),
        scratch_shapes=scratch,
        compiler_params=pltpu.CompilerParams(
            collective_id=0, has_side_effects=True, vmem_limit_bytes=56 * 1024 * 1024
        ),
    )(
        master,
        grad_out.reshape(grad_out.shape[1:]),
        pre_mid.reshape(pre_mid.shape[1:]),
        pre_up.reshape(pre_up.shape[1:]),
        coarse_in.reshape(2, 2, 32, 256),
    )
    mean_grad = summed / 8.0
    new_moment = beta_one * moment + (1.0 - beta_one) * mean_grad
    new_second = beta_two * second + (1.0 - beta_two) * mean_grad * mean_grad
    corrected = new_moment / (1.0 - beta_one**adam_step)
    scaled = jnp.sqrt(new_second / (1.0 - beta_two**adam_step)) + adam_eps
    new_master = master - learn_rate * corrected / scaled
    return (coarse_grad.reshape(coarse_in.shape), new_master, new_moment, new_second)


def solution(mesh):
    wide = P("dp", None, "slab", None, None, None)
    flat = P(("slab", "dp"), None)
    return jax.shard_map(
        body,
        mesh=mesh,
        in_specs=(wide, wide, wide, wide, flat, flat, flat),
        out_specs=(wide, flat, flat, flat),
        check_vma=False,
    )
```

```python
import jax
import jax.numpy as jnp
from jax import lax
from jax.experimental import pallas as pl
from jax.experimental.pallas import tpu as pltpu
from jax.sharding import PartitionSpec as P

beta_one = 0.9
beta_two = 0.999
adam_step = 10.0
learn_rate = 0.01
adam_eps = 1e-08

F32 = jnp.float32
BF16 = jnp.bfloat16
MESH = pl.DeviceIdType.MESH

ROWS = 108
TOTAL = 13824
FILTER = 3456
START = (0, 48, 80)
HOLD = (48, 32, 32)
VALID = (48, 32, 28)
ORDER = (("y", "z", "x"), ("y", "x", "z"), ("z", "x", "y"))
EARLY, LATE = 0, 1


def nt(left, right):
    return lax.dot_general(
        left, right, (((1,), (1,)), ((), ())), preferred_element_type=F32
    )


def nn(left, right):
    return jnp.dot(left, right, preferred_element_type=F32)


def kernel(
    master_in, grad_out_in, pre_mid_in, pre_up_in, coarse_in,
    coarse_grad, summed,
    master, grad_out, pre_mid, pre_up, coarse,
    g0, g1, g2, sb0, sb1, sb2, rb0, rb1, rb2, t0, t1, t2, ra0, ra1, ra2,
    u0, u1, u2, rc0, rc1, rc2, v0, v1, v2, rd0, rd1, rd2,
    wflat, fflat, w_one, w_two, w_up, x_out, x_mid, act_mid, act_up, mid_raw, up_raw, up_before,
    gathered, lowest, halo_out, halo_mid, halo_up,
    ag_send, ag_recv, core_send, core_recv, rs_send, rs_recv, swap_send, swap_recv,
    halo_send, halo_recv, load_sem, token_sem,
):
    gat, sbs, rbs, tot = (g0, g1, g2), (sb0, sb1, sb2), (rb0, rb1, rb2), (t0, t1, t2)
    ras, us, rcs, vs, rds = (
        (ra0, ra1, ra2), (u0, u1, u2), (rc0, rc1, rc2), (v0, v1, v2), (rd0, rd1, rd2),
    )
    slab, dp = lax.axis_index("slab"), lax.axis_index("dp")
    at = {
        "x": lax.rem(slab // 4, 4),
        "y": (slab // 16) * 2 + dp // 2,
        "z": lax.rem(slab, 4),
    }
    core = lax.rem(dp, 2)
    other = 1 - core

    def device(where, which):
        return (
            (where["y"] // 2) * 16 + where["x"] * 4 + where["z"],
            lax.rem(where["y"], 2) * 2 + which,
        )

    def moved(axis, step):
        where = dict(at)
        where[axis] = lax.rem(at[axis] + step, 4)
        return where

    def ahead(axis, step):
        return device(moved(axis, step), core)

    partner = device(at, other)
    after = (lax.rem(slab + 1, 32), dp)
    before = (lax.rem(slab + 31, 32), dp)

    def copy(src, dst, send, recv, target):
        return pltpu.make_async_remote_copy(
            src_ref=src, dst_ref=dst, send_sem=send, recv_sem=recv,
            device_id=target, device_id_type=MESH,
        )

    barrier = pltpu.get_barrier_semaphore()
    targets = [partner]
    targets += [ahead(axis, step) for axis in ("x", "y", "z") for step in (1, 2, 3)]
    for target in targets:
        pl.semaphore_signal(barrier, inc=1, device_id=target, device_id_type=MESH)

    def block(ref, part, lead, where):
        axes = ORDER[part]
        if part == 2:
            inner = [lax.rem(where["y"], 2), where["x"], where["z"]]
        else:
            inner = [where[axes[2]], where[axes[1]], lax.rem(where["y"], 2)]
        return tuple([where["y"] // 2] + lead + inner)

    loads = [
        pltpu.make_async_copy(src, dst, load_sem.at[number])
        for number, (src, dst) in enumerate(
            (
                (master_in, master),
                (grad_out_in, grad_out),
                (pre_mid_in, pre_mid),
                (pre_up_in, pre_up),
                (coarse_in, coarse.at[0, :, 0:2]),
            )
        )
    ]
    for load in loads:
        load.start()

    loads[0].wait()
    for part in range(3):
        rows = master[START[part] : START[part] + VALID[part], :]
        if HOLD[part] > VALID[part]:
            rows = jnp.concatenate(
                [rows, jnp.zeros((HOLD[part] - VALID[part], 128), F32)], axis=0
            )
        gat[part][block(gat[part], part, [core], at)] = rows.astype(BF16)
    pl.semaphore_wait(barrier, len(targets))

    started = []

    def go(c):
        c.start()
        started.append(c)
        return c

    def piece(part, which, level, half, where):
        place = block(gat[part], part, [which], where)
        if part == 2:
            return gat[part].at[place[: 5 - level]]
        if level == 0:
            return gat[part].at[place]
        return gat[part].at[(half,) + place[1 : 5 - level]]

    def back_half(step):
        return lax.rem(at["y"] + 4 - step, 4) // 2

    def gather(part, level, half):
        axis = ORDER[part][level]
        out = []
        for step in (1, 3, 2):
            sem = (part, level, step - 1, half)
            src = piece(part, core, level, half, at)
            go(copy(src, src, ag_send.at[sem], ag_recv.at[sem], ahead(axis, step)))
            dst = piece(part, core, level, half, moved(axis, 4 - step))
            out.append(copy(dst, dst, ag_send.at[sem], ag_recv.at[sem], partner))
        return out

    tall_half = at["y"] // 2
    tall = []
    for step in (1, 3, 2):
        sem = (2, 2, step - 1, 0)
        src = piece(2, core, 2, 0, at)
        dst = piece(2, core, 2, 0, moved("y", 4 - step))
        tall.append(
            (
                step,
                back_half(step),
                copy(src, src, ag_send.at[sem], ag_recv.at[sem], ahead("y", step)),
                copy(dst, dst, ag_send.at[sem], ag_recv.at[sem], partner),
            )
        )

    def tall_start(half):
        for _, _, c, _ in tall:
            pl.when(tall_half == half)(c.start)

    def tall_forward(half):
        for step, owner, _, c in tall:

            @pl.when(owner == half)
            def _():
                c.wait_recv()
                core_copy(2, 0, step, core).start()

    def tall_partner(half):
        for step, owner, _, _ in tall:
            pl.when(owner == half)(core_copy(2, 0, step, other).wait_recv)

    def core_copy(part, half, number, which):
        axis = ORDER[part][2]
        ref = piece(part, which, 2, half, moved(axis, 4 - number))
        sem = (part, half, number)
        return copy(ref, ref, core_send.at[sem], core_recv.at[sem], partner)

    def wait_for(copies):
        for c in copies:
            c.wait_recv()

    leg = [gather(part, 0, EARLY) for part in range(3)]
    for step in (1, 3, 2):
        pl.semaphore_signal(token_sem.at[0], inc=1, device_id=ahead("z", step), device_id_type=MESH)

    row = lax.broadcasted_iota(jnp.int32, (128, 128), 0)
    lane = lax.broadcasted_iota(jnp.int32, (128, 128), 1)
    breadth = lax.rem(row, 16)
    for ext in (x_out, x_mid):
        ext[:, :, 0] = jnp.zeros((2, 6, 16, 384), BF16)
        ext[:, :, 9] = jnp.zeros((2, 6, 16, 384), BF16)
    fflat[TOTAL : TOTAL + 8, :] = jnp.zeros((8, 128), F32)

    def widen(ext, sample, layer, value):
        later = jnp.where(breadth == 15, 0.0, pltpu.roll(value, 127, 0))
        earlier = jnp.where(breadth == 0, 0.0, pltpu.roll(value, 1, 0))
        wide = jnp.concatenate(
            [later.astype(BF16), value.astype(BF16), earlier.astype(BF16)], axis=1
        )
        ext[sample, layer, 1:9] = wide.reshape(8, 16, 384)

    def turn(act_t, first, value):
        turned = jnp.maximum(value, 0.0).T
        columns = slice(first * 128, first * 128 + 128)
        low = jnp.where(lane < 16, 0.0, pltpu.roll(turned, 16, 1))
        high = jnp.where(lane >= 112, 0.0, pltpu.roll(turned, 112, 1))
        act_t[0:128, columns] = low.astype(BF16)
        act_t[128:256, columns] = turned.astype(BF16)
        act_t[256:384, columns] = high.astype(BF16)

    def transposed_act(act_t, pre, depth, first):
        for sample in range(2):
            for layer in range(4):
                value = pre[sample, layer].reshape(128, 128).astype(F32)
                turn(act_t, sample * depth + first + layer, value)

    def transposed_edges(act_t, halo):
        for sample in range(2):
            low = halo[0, sample].reshape(128, 128).astype(F32)
            turn(act_t, sample * 6, jnp.where(slab > 0, low, 0.0))
            high = halo[1, sample].reshape(128, 128).astype(F32)
            turn(act_t, sample * 6 + 5, jnp.where(slab < 31, high, 0.0))

    def own_layers(index, carry):
        sample, layer = index // 4, lax.rem(index, 4)
        widen(x_out, sample, layer + 1, grad_out[sample, layer].reshape(128, 128).astype(F32))
        return carry

    def edges(ext, halo):
        for sample in range(2):
            low = halo[0, sample].reshape(128, 128).astype(F32)
            widen(ext, sample, 0, jnp.where(slab > 0, low, 0.0))
            high = halo[1, sample].reshape(128, 128).astype(F32)
            widen(ext, sample, 5, jnp.where(slab < 31, high, 0.0))

    def grad_by_cotangent(ext, act_t, first, depth):
        right = ext[:, 2 - depth : 6 - depth, 1:9].reshape(1024, 384)
        store_grad(first, depth, nn(act_t[...], right))

    def grad_by_act(ext, act_t, first, depth):
        out = jnp.zeros((384, 384), F32)
        for sample in range(2):
            start = (sample * 6 + depth) * 128
            out = out + nn(act_t[:, start : start + 512], ext[sample, 1:5, 1:9].reshape(512, 384))
        store_grad(first, depth, out)

    def store_grad(first, depth, out):
        for height in range(3):
            for col in range(3):
                start = first + ((depth * 3 + height) * 3 + col) * 128
                fflat[start : start + 128, :] = out[
                    height * 128 : height * 128 + 128, col * 128 : col * 128 + 128
                ]

    def back_conv(ext, weight, layers):
        acc = jnp.zeros((512, 128), F32)
        for depth in range(3):
            for height in range(3):
                rows = slice(2 - height, 10 - height)
                left = jnp.concatenate(
                    [ext[:, layer + 2 - depth, rows].reshape(256, 384) for layer in layers], axis=0
                )
                acc = acc + nt(left, weight[depth * 3 + height])
        return acc

    def place(chip):
        return {"x": lax.rem(chip // 8, 4), "y": (chip // 32) * 2 + lax.rem(chip, 2), "z": lax.rem(chip // 2, 4)}

    def unpack(chip, carry):
        where = place(chip)
        base = pl.multiple_of(chip * 216, 8)
        pieces = []
        for which in range(2):
            for part in range(3):
                value = gat[part][block(gat[part], part, [which], where)]
                pieces.append(value.astype(F32)[: VALID[part]])
        wflat[pl.ds(base, 216), :] = jnp.concatenate(pieces, axis=0)
        return carry

    def taps(weight, first, width):
        def one(index, carry):
            for col in range(3):
                start = pl.multiple_of((index * 3 + col) * width + first, 128)
                weight[index, :, col * 128 : col * 128 + 128] = wflat[pl.ds(start, width), :].astype(BF16)
            return carry

        lax.fori_loop(0, 9, one, 0)

    def pack(chip, carry):
        where = place(chip)
        base = pl.multiple_of(chip * 216, 8)
        value = fflat[pl.ds(base, 224), :]
        for which in range(2):
            for part in range(3):
                start = which * ROWS + START[part]
                rows = value[start : start + HOLD[part]].astype(BF16)
                sbs[part][block(sbs[part], part, [which], where)[1:]] = rows
        return carry

    def pack_late(chip, carry):
        where = place(chip)
        base = pl.multiple_of(chip * 216, 8)
        value = fflat[pl.ds(base, 224), :]
        value = jnp.where(core == 0, value[0:112], value[ROWS : ROWS + 112])
        for part in range(3):
            rows = value[START[part] : START[part] + HOLD[part]].astype(BF16)
            tot[part][block(tot[part], part, [], where)] = rows
        return carry

    def swap(first):
        out = []
        for part in range(3):
            group = pl.ds(first, 2)
            if part == 0:
                src, dst = sbs[0].at[other, group], rbs[0].at[group]
            else:
                src, dst = sbs[part].at[other, :, group], rbs[part].at[:, group]
            sem = (part, first // 2)
            out.append(go(copy(src, dst, swap_send.at[sem], swap_recv.at[sem], partner)))
        return out

    def core_sums(first, swapped):
        for part in range(3):
            swapped[part].wait_recv()

            def add(index, carry, part=part):
                if part == 0:
                    a, b = first + index // 4, lax.rem(index, 4)
                else:
                    a, b = index // 2, first + lax.rem(index, 2)
                total = sbs[part][core, a, b].astype(F32) + rbs[part][a, b].astype(F32)
                tot[part][EARLY, a, b] = total.astype(BF16)
                return carry

            lax.fori_loop(0, (8, 8, 4)[part], add, 0)

    def scatter(part, level, src, dst, sems):
        axis = ORDER[part][2 - level]
        out = []
        for step in (1, 3, 2):
            sem = (part, level, step - 1, sems)
            out.append(
                go(
                    copy(
                        src.at[lax.rem(at[axis] + step, 4)], dst.at[step - 1],
                        rs_send.at[sem], rs_recv.at[sem], ahead(axis, step),
                    )
                )
            )
        return out

    early_x, early_z, column = [], [], []
    for step in (1, 3, 2):
        where = moved("x", step)
        sem = (0, 0, step - 1, 0)
        c = copy(
            tot[0].at[EARLY, where["x"]], ras[0].at[EARLY, step - 1],
            rs_send.at[sem], rs_recv.at[sem], device(where, core),
        )
        early_x.append((where["x"] // 2 * 2, c))
        where = moved("y", step)
        owner = where["y"] // 2
        for number, group in enumerate((pl.ds(2, 2), pl.ds(0, 2), pl.ds(0, 4))):
            sem = (2, 0, step - 1, number)
            c = copy(
                tot[2].at[where["y"] // 2, lax.rem(where["y"], 2), group],
                ras[2].at[step - 1, group],
                rs_send.at[sem], rs_recv.at[sem], device(where, core),
            )
            column.append((number, owner, c))

    def early_sends(first):
        number = 1 - first // 2
        for owner, c in early_x:
            pl.when(owner == first)(c.start)
        group = pl.ds(first, 2)
        for step in (1, 3, 2):
            where = moved("z", step)
            sem = (1, 0, step - 1, number)
            early_z.append(
                go(
                    copy(
                        tot[1].at[EARLY, where["z"], group], ras[1].at[EARLY, step - 1, group],
                        rs_send.at[sem], rs_recv.at[sem], device(where, core),
                    )
                )
            )
        for which, owner, c in column:
            if which == number:
                pl.when(owner == EARLY)(c.start)

    def late_sends():
        out = [scatter(part, 0, tot[part].at[LATE], ras[part].at[LATE], 2) for part in range(2)]
        for which, owner, c in column:
            if which == 2:
                pl.when(owner == LATE)(c.start)
        return out

    for load in loads[1:]:
        load.wait()
    transposed_act(act_mid, pre_mid, 4, 0)
    for part in range(3):
        wait_for(leg[part])
    leg = [gather(part, 1, EARLY) for part in range(3)]
    pl.semaphore_wait(token_sem.at[0], 3)
    pl.semaphore_signal(token_sem.at[1], inc=1, device_id=ahead("y", 2), device_id_type=MESH)
    lax.fori_loop(0, 8, own_layers, 0)
    grad_by_cotangent(x_out, act_mid, FILTER, 1)
    pl.semaphore_wait(token_sem.at[1], 1)
    halos = []
    for number, (src, dst, target) in enumerate(
        (
            (grad_out.at[:, 3], halo_out.at[0], after),
            (grad_out.at[:, 0], halo_out.at[1], before),
            (pre_up.at[:, 3], halo_up.at[0], after),
            (pre_up.at[:, 0], halo_up.at[1], before),
            (coarse.at[0, :, 0], coarse.at[0, :, 2], before),
        )
    ):
        sem = 3 + number
        halos.append(go(copy(src, dst, halo_send.at[sem], halo_recv.at[sem], target)))
    third = []
    for part in (2, 0, 1):
        wait_for(leg[part])
        if part == 2:
            tall_start(EARLY)
        else:
            third.append(gather(part, 2, EARLY))
        go(core_copy(part, EARLY, 0, core))
    leg = [gather(part, 1, LATE) for part in range(2)]
    transposed_act(act_up, pre_up, 6, 1)
    wait_for(halos[0:2])
    edges(x_out, halo_out)
    grad_by_cotangent(x_out, act_mid, FILTER, 0)
    grad_by_cotangent(x_out, act_mid, FILTER, 2)
    lax.fori_loop(16, 32, pack, 0)
    two_swap = swap(2)

    def forward(part, half, copies):
        for step, c in zip((1, 3, 2), copies):
            c.wait_recv()
            go(core_copy(part, half, step, core))

    tall_forward(EARLY)
    for part in range(2):
        forward(part, EARLY, third[part])
    third = []
    for part in range(2):
        wait_for(leg[part])
        third.append(gather(part, 2, LATE))
        go(core_copy(part, LATE, 0, core))
    tall_start(LATE)
    core_copy(2, EARLY, 0, other).wait_recv()
    tall_partner(EARLY)
    for part in range(2):
        wait_for([core_copy(part, EARLY, number, other) for number in range(4)])

    lax.fori_loop(16, 32, unpack, 0)
    taps(w_two, FILTER, 128)

    def mid_layers(layers):
        both = back_conv(x_out, w_two, layers)
        for number, layer in enumerate(layers):
            value = both[number * 256 : number * 256 + 256]
            keep = pre_mid[:, layer].reshape(256, 128).astype(F32) > 0.0
            value = jnp.where(keep, value, 0.0).astype(BF16)
            mid_raw[:, layer] = value.reshape(2, 8, 16, 128)
            for sample in range(2):
                widen(x_mid, sample, layer + 1, value[sample * 128 : sample * 128 + 128].astype(F32))

    mid_layers((3, 0))
    mid_up = go(copy(mid_raw.at[:, 3], halo_mid.at[0], halo_send.at[0], halo_recv.at[0], after))
    mid_down = go(copy(mid_raw.at[:, 0], halo_mid.at[1], halo_send.at[1], halo_recv.at[1], before))
    core_sums(2, two_swap)
    early_sends(2)
    mid_layers((1, 2))
    lax.fori_loop(0, 16, unpack, 0)
    taps(w_one, 0, 128)
    wait_for(halos[2:])
    pair = go(copy(coarse.at[0], coarse.at[1], halo_send.at[8], halo_recv.at[8], partner))
    transposed_edges(act_up, halo_up)
    for depth in range(3):
        grad_by_act(x_mid, act_up, 0, depth)
    lax.fori_loop(0, 16, pack, 0)
    one_swap = swap(0)
    tall_forward(LATE)
    for part in range(2):
        forward(part, LATE, third[part])
    mid_up.wait_recv()
    mid_down.wait_recv()
    core_sums(0, one_swap)
    early_sends(0)
    edges(x_mid, halo_mid)

    for layers in ((3, 0), (1, 2)):
        both = back_conv(x_mid, w_one, layers)
        for number, layer in enumerate(layers):
            value = both[number * 256 : number * 256 + 256]
            keep = pre_up[:, layer].reshape(256, 128).astype(F32) > 0.0
            value = jnp.where(keep, value, 0.0).astype(BF16)
            up_raw[0, :, layer] = value.reshape(2, 128, 128)
    up_pair = go(copy(up_raw.at[0], up_raw.at[1], halo_send.at[2], halo_recv.at[2], partner))
    up_next = go(copy(up_raw.at[0, :, 3], up_before, halo_send.at[9], halo_recv.at[9], after))

    def second_sums(part, half, copies):
        wait_for(copies)
        mine = at[ORDER[part][2]]

        def add(index, carry):
            total = tot[part][half, mine, index].astype(F32)
            for step in range(3):
                total = total + ras[part][half, step, index].astype(F32)
            us[part][half, index] = total.astype(BF16)
            return carry

        lax.fori_loop(0, 4, add, 0)
        return scatter(part, 1, us[part].at[half], rcs[part].at[half], half)

    def third_sums(part, half, copies):
        wait_for(copies)
        total = us[part][half, at[ORDER[part][1]]].astype(F32)
        for step in range(3):
            total = total + rcs[part][half, step].astype(F32)
        vs[part][2 * half : 2 * half + 2] = total.astype(BF16)

    pick_row = lax.broadcasted_iota(jnp.int32, (288, 128), 0)
    pick_lane = lax.broadcasted_iota(jnp.int32, (288, 128), 1)
    tap, coarse_row, coarse_col = pick_row // 32, lax.rem(pick_row // 8, 4), lax.rem(pick_row, 8)
    fine_row = 2 * coarse_row + tap // 3 - 1
    fine_col = 2 * coarse_col + lax.rem(tap, 3) - 1
    chosen = (fine_row >= 0) & (fine_col >= 0) & (pick_lane == fine_row * 16 + fine_col)
    pick = jnp.where(chosen, 1.0, 0.0).astype(BF16)

    def spread(slot, sample, layer):
        picked = nn(pick, up_raw[slot, sample, layer]).astype(BF16)
        first = ((slot * 2 + sample) * 2 + layer // 2) * 32
        for depth in (1,) if layer % 2 == 0 else (0, 2):
            for tap in range(9):
                columns = slice((depth * 9 + tap) * 128, (depth * 9 + tap) * 128 + 128)
                gathered[first : first + 32, columns] = picked[tap * 32 : tap * 32 + 32]
        return picked

    def lower(sample, quarter, picked):
        first = (sample * 2 + quarter) * 32
        for tap in range(9):
            lowest[first : first + 32, tap * 128 : tap * 128 + 128] = picked[tap * 32 : tap * 32 + 32]

    for sample in range(2):
        for layer in range(4):
            picked = spread(0, sample, layer)
            if layer == 1:
                lower(sample, 1, picked)
    pair.wait_recv()
    turned = []
    for first in (1, 0):
        rows = []
        for slot in range(2):
            for sample in range(2):
                for quarter in (first, first + 1):
                    value = coarse[slot, sample, quarter].astype(F32)
                    if quarter == 2:
                        value = jnp.where(slab < 31, value, 0.0)
                    rows.append(value)
        turned.append(jnp.concatenate(rows, axis=0).T.astype(BF16))
    up_pair.wait_recv()
    for sample in range(2):
        for layer in range(4):
            spread(1, sample, layer)
    for index in range(9):
        out = nn(turned[min(index // 3, 1)], gathered[:, index * 384 : index * 384 + 384])
        for col in range(3):
            start = 2 * FILTER + (index * 3 + col) * 256
            fflat[start : start + 256, :] = out[:, col * 128 : col * 128 + 128]
    lax.fori_loop(32, 64, pack_late, 0)
    late_first = late_sends()
    early_first = ([c for _, c in early_x], early_z)

    tall_partner(LATE)
    for part in range(2):
        wait_for([core_copy(part, LATE, number, other) for number in range(4)])
    early_second = [second_sums(part, EARLY, early_first[part]) for part in range(2)]
    lax.fori_loop(32, 64, unpack, 0)
    taps(w_up, 2 * FILTER, 256)
    up_next.wait_recv()
    for sample in range(2):
        value = jnp.where(slab > 0, up_before[sample].astype(F32), 0.0).astype(BF16)
        lower(sample, 0, nn(pick, value).astype(BF16))
    acc = jnp.zeros((128, 256), F32)
    for index in range(9):
        if index < 3:
            left = lowest[:, index * 384 : index * 384 + 384]
        else:
            left = gathered[0:128, index * 384 : index * 384 + 384]
        acc = acc + nt(left, w_up[index])
    coarse_grad[...] = acc.astype(BF16)
    for part in range(2):
        third_sums(part, EARLY, early_second[part])

    for which, _, c in column:
        pl.when(tall_half == (LATE if which == 2 else EARLY))(c.wait_recv)
    mine = (at["y"] // 2, lax.rem(at["y"], 2))

    def add_plane(index, carry):
        total = tot[2][mine[0], mine[1], index].astype(F32)
        for step in range(3):
            total = total + ras[2][step, index].astype(F32)
        us[2][index] = total.astype(BF16)
        return carry

    lax.fori_loop(0, 4, add_plane, 0)
    plane = scatter(2, 1, us[2], rcs[2], 0)
    late_second = [second_sums(part, LATE, late_first[part]) for part in range(2)]
    wait_for(plane)
    total = us[2][at["x"]].astype(F32)
    for step in range(3):
        total = total + rcs[2][step].astype(F32)
    vs[2][...] = total.astype(BF16)
    last = [None, None, scatter(2, 2, vs[2], rds[2], 0)]
    for part in range(2):
        third_sums(part, LATE, late_second[part])
        last[part] = scatter(part, 2, vs[part], rds[part], 0)
    for part in (2, 0, 1):
        wait_for(last[part])
        total = vs[part][at[ORDER[part][0]]].astype(F32)
        for step in range(3):
            total = total + rds[part][step].astype(F32)
        summed[START[part] : START[part] + VALID[part], :] = total[: VALID[part]]
    for c in started:
        c.wait_send()
    for _, c in early_x:
        c.wait_send()
    for which, owner, c in column:
        pl.when(owner == (LATE if which == 2 else EARLY))(c.wait_send)
    for step, _, c, _ in tall:
        c.wait_send()
        core_copy(2, 0, step, core).wait_send()


def body(coarse_in, pre_up, pre_mid, grad_out, master, moment, second):
    vmem = pl.BlockSpec(memory_space=pltpu.VMEM)
    held = pl.BlockSpec(memory_space=pl.ANY)
    scratch = [
        pltpu.VMEM((ROWS, 128), F32),
        pltpu.VMEM((2, 4, 8, 16, 128), BF16),
        pltpu.VMEM((2, 4, 8, 16, 128), BF16),
        pltpu.VMEM((2, 4, 8, 16, 128), BF16),
        pltpu.VMEM((2, 2, 3, 32, 256), BF16),
    ]
    for shape, column in (
        ((2, 2, 4, 4, 2), (2, 2, 2, 4, 4)),
        ((2, 4, 4, 2), (2, 2, 4, 4)),
        ((4, 4, 2), (2, 4, 4)),
        ((2, 4, 4, 2), (2, 2, 4, 4)),
        ((2, 3, 4, 2), (3, 4, 4)),
        ((2, 4, 2), (4, 4)),
        ((2, 3, 2), (3, 4)),
        ((4,), (4,)),
        ((3,), (3,)),
    ):
        for part in range(3):
            lead = column if part == 2 else shape
            scratch.append(pltpu.VMEM(lead + (HOLD[part], 128), BF16))
    scratch += [
        pltpu.VMEM((TOTAL, 128), F32),
        pltpu.VMEM((TOTAL + 8, 128), F32),
        pltpu.VMEM((9, 128, 384), BF16),
        pltpu.VMEM((9, 128, 384), BF16),
        pltpu.VMEM((9, 256, 384), BF16),
        pltpu.VMEM((2, 6, 10, 16, 384), BF16),
        pltpu.VMEM((2, 6, 10, 16, 384), BF16),
        pltpu.VMEM((384, 1024), BF16),
        pltpu.VMEM((384, 1536), BF16),
        pltpu.VMEM((2, 4, 8, 16, 128), BF16),
        pltpu.VMEM((2, 2, 4, 128, 128), BF16),
        pltpu.VMEM((2, 128, 128), BF16),
        pltpu.VMEM((256, FILTER), BF16),
        pltpu.VMEM((128, 9 * 128), BF16),
        pltpu.VMEM((2, 2, 8, 16, 128), BF16),
        pltpu.VMEM((2, 2, 8, 16, 128), BF16),
        pltpu.VMEM((2, 2, 8, 16, 128), BF16),
    ]
    for shape in ((3, 3, 3, 2), (3, 2, 4), (3, 3, 3, 3), (3, 2), (10,)):
        scratch += [pltpu.SemaphoreType.DMA(shape)] * 2
    scratch += [pltpu.SemaphoreType.DMA((5,)), pltpu.SemaphoreType.REGULAR((2,))]
    coarse_grad, summed = pl.pallas_call(
        kernel,
        out_shape=(
            jax.ShapeDtypeStruct((128, 256), BF16),
            jax.ShapeDtypeStruct((ROWS, 128), F32),
        ),
        in_specs=[held] * 5,
        out_specs=(vmem, vmem),
        scratch_shapes=scratch,
        compiler_params=pltpu.CompilerParams(
            collective_id=0, has_side_effects=True, vmem_limit_bytes=56 * 1024 * 1024
        ),
    )(
        master,
        grad_out.reshape(grad_out.shape[1:]),
        pre_mid.reshape(pre_mid.shape[1:]),
        pre_up.reshape(pre_up.shape[1:]),
        coarse_in.reshape(2, 2, 32, 256),
    )
    mean_grad = summed / 8.0
    new_moment = beta_one * moment + (1.0 - beta_one) * mean_grad
    new_second = beta_two * second + (1.0 - beta_two) * mean_grad * mean_grad
    corrected = new_moment / (1.0 - beta_one**adam_step)
    scaled = jnp.sqrt(new_second / (1.0 - beta_two**adam_step)) + adam_eps
    new_master = master - learn_rate * corrected / scaled
    return (coarse_grad.reshape(coarse_in.shape), new_master, new_moment, new_second)


def solution(mesh):
    wide = P("dp", None, "slab", None, None, None)
    flat = P(("slab", "dp"), None)
    return jax.shard_map(
        body,
        mesh=mesh,
        in_specs=(wide, wide, wide, wide, flat, flat, flat),
        out_specs=(wide, flat, flat, flat),
        check_vma=False,
    )
```

```python
import jax
import jax.numpy as jnp
from jax import lax
from jax.experimental import pallas as pl
from jax.experimental.pallas import tpu as pltpu
from jax.sharding import PartitionSpec as P

beta_one = 0.9
beta_two = 0.999
adam_step = 10.0
learn_rate = 0.01
adam_eps = 1e-08

F32 = jnp.float32
BF16 = jnp.bfloat16
MESH = pl.DeviceIdType.MESH

ROWS = 108
TOTAL = 13824
FILTER = 3456
START = (0, 48, 80)
HOLD = (48, 32, 32)
VALID = (48, 32, 28)
ORDER = (("y", "z", "x"), ("y", "x", "z"), ("z", "x", "y"))
EARLY, LATE = 0, 1


def nt(left, right):
    return lax.dot_general(
        left, right, (((1,), (1,)), ((), ())), preferred_element_type=F32
    )


def nn(left, right):
    return jnp.dot(left, right, preferred_element_type=F32)


def kernel(
    master_in, grad_out_in, pre_mid_in, pre_up_in, coarse_in,
    coarse_grad, summed,
    master, grad_out, pre_mid, pre_up, coarse,
    g0, g1, g2, sb0, sb1, sb2, rb0, rb1, rb2, t0, t1, t2, ra0, ra1, ra2,
    u0, u1, u2, rc0, rc1, rc2, v0, v1, v2, rd0, rd1, rd2,
    wflat, fflat, w_one, w_two, w_up, x_out, x_mid, act_mid, act_up, mid_raw, up_raw, up_before,
    gathered, lowest, halo_out, halo_mid, halo_up,
    ag_send, ag_recv, core_send, core_recv, rs_send, rs_recv, swap_send, swap_recv,
    halo_send, halo_recv, load_sem, token_sem,
):
    gat, sbs, rbs, tot = (g0, g1, g2), (sb0, sb1, sb2), (rb0, rb1, rb2), (t0, t1, t2)
    ras, us, rcs, vs, rds = (
        (ra0, ra1, ra2), (u0, u1, u2), (rc0, rc1, rc2), (v0, v1, v2), (rd0, rd1, rd2),
    )
    slab, dp = lax.axis_index("slab"), lax.axis_index("dp")
    at = {
        "x": lax.rem(slab // 4, 4),
        "y": (slab // 16) * 2 + dp // 2,
        "z": lax.rem(slab, 4),
    }
    core = lax.rem(dp, 2)
    other = 1 - core

    def device(where, which):
        return (
            (where["y"] // 2) * 16 + where["x"] * 4 + where["z"],
            lax.rem(where["y"], 2) * 2 + which,
        )

    def moved(axis, step):
        where = dict(at)
        where[axis] = lax.rem(at[axis] + step, 4)
        return where

    def ahead(axis, step):
        return device(moved(axis, step), core)

    partner = device(at, other)
    after = (lax.rem(slab + 1, 32), dp)
    before = (lax.rem(slab + 31, 32), dp)

    def copy(src, dst, send, recv, target):
        return pltpu.make_async_remote_copy(
            src_ref=src, dst_ref=dst, send_sem=send, recv_sem=recv,
            device_id=target, device_id_type=MESH,
        )

    barrier = pltpu.get_barrier_semaphore()
    targets = [partner]
    targets += [ahead(axis, step) for axis in ("x", "y", "z") for step in (1, 2, 3)]
    for target in targets:
        pl.semaphore_signal(barrier, inc=1, device_id=target, device_id_type=MESH)

    def block(ref, part, lead, where):
        axes = ORDER[part]
        if part == 2:
            inner = [lax.rem(where["y"], 2), where["x"], where["z"]]
        else:
            inner = [where[axes[2]], where[axes[1]], lax.rem(where["y"], 2)]
        return tuple([where["y"] // 2] + lead + inner)

    loads = [
        pltpu.make_async_copy(src, dst, load_sem.at[number])
        for number, (src, dst) in enumerate(
            (
                (master_in, master),
                (grad_out_in, grad_out),
                (pre_mid_in, pre_mid),
                (pre_up_in, pre_up),
                (coarse_in, coarse.at[0, :, 0:2]),
            )
        )
    ]
    for load in loads:
        load.start()

    loads[0].wait()
    for part in range(3):
        rows = master[START[part] : START[part] + VALID[part], :]
        if HOLD[part] > VALID[part]:
            rows = jnp.concatenate(
                [rows, jnp.zeros((HOLD[part] - VALID[part], 128), F32)], axis=0
            )
        gat[part][block(gat[part], part, [core], at)] = rows.astype(BF16)
    pl.semaphore_wait(barrier, len(targets))

    started = []

    def go(c):
        c.start()
        started.append(c)
        return c

    def piece(part, which, level, half, where):
        place = block(gat[part], part, [which], where)
        if part == 2:
            return gat[part].at[place[: 5 - level]]
        if level == 0:
            return gat[part].at[place]
        return gat[part].at[(half,) + place[1 : 5 - level]]

    def back_half(step):
        return lax.rem(at["y"] + 4 - step, 4) // 2

    def gather(part, level, half):
        axis = ORDER[part][level]
        out = []
        for step in (1, 3, 2):
            sem = (part, level, step - 1, half)
            src = piece(part, core, level, half, at)
            go(copy(src, src, ag_send.at[sem], ag_recv.at[sem], ahead(axis, step)))
            dst = piece(part, core, level, half, moved(axis, 4 - step))
            out.append(copy(dst, dst, ag_send.at[sem], ag_recv.at[sem], partner))
        return out

    tall_half = at["y"] // 2
    tall = []
    for step in (1, 3, 2):
        sem = (2, 2, step - 1, 0)
        src = piece(2, core, 2, 0, at)
        dst = piece(2, core, 2, 0, moved("y", 4 - step))
        tall.append(
            (
                step,
                back_half(step),
                copy(src, src, ag_send.at[sem], ag_recv.at[sem], ahead("y", step)),
                copy(dst, dst, ag_send.at[sem], ag_recv.at[sem], partner),
            )
        )

    def tall_start(half):
        for _, _, c, _ in tall:
            pl.when(tall_half == half)(c.start)

    def tall_forward(half):
        for step, owner, _, c in tall:

            @pl.when(owner == half)
            def _():
                c.wait_recv()
                core_copy(2, 0, step, core).start()

    def tall_partner(half):
        for step, owner, _, _ in tall:
            pl.when(owner == half)(core_copy(2, 0, step, other).wait_recv)

    def core_copy(part, half, number, which):
        axis = ORDER[part][2]
        ref = piece(part, which, 2, half, moved(axis, 4 - number))
        sem = (part, half, number)
        return copy(ref, ref, core_send.at[sem], core_recv.at[sem], partner)

    def wait_for(copies):
        for c in copies:
            c.wait_recv()

    leg = [gather(part, 0, EARLY) for part in range(3)]
    for step in (1, 3, 2):
        pl.semaphore_signal(token_sem.at[0], inc=1, device_id=ahead("z", step), device_id_type=MESH)

    row = lax.broadcasted_iota(jnp.int32, (128, 128), 0)
    lane = lax.broadcasted_iota(jnp.int32, (128, 128), 1)
    breadth = lax.rem(row, 16)
    for ext in (x_out, x_mid):
        ext[:, :, 0] = jnp.zeros((2, 6, 16, 384), BF16)
        ext[:, :, 9] = jnp.zeros((2, 6, 16, 384), BF16)
    fflat[TOTAL : TOTAL + 8, :] = jnp.zeros((8, 128), F32)

    def widen(ext, sample, layer, value):
        later = jnp.where(breadth == 15, 0.0, pltpu.roll(value, 127, 0))
        earlier = jnp.where(breadth == 0, 0.0, pltpu.roll(value, 1, 0))
        wide = jnp.concatenate(
            [later.astype(BF16), value.astype(BF16), earlier.astype(BF16)], axis=1
        )
        ext[sample, layer, 1:9] = wide.reshape(8, 16, 384)

    def turn(act_t, first, value):
        turned = jnp.maximum(value, 0.0).T
        columns = slice(first * 128, first * 128 + 128)
        low = jnp.where(lane < 16, 0.0, pltpu.roll(turned, 16, 1))
        high = jnp.where(lane >= 112, 0.0, pltpu.roll(turned, 112, 1))
        act_t[0:128, columns] = low.astype(BF16)
        act_t[128:256, columns] = turned.astype(BF16)
        act_t[256:384, columns] = high.astype(BF16)

    def transposed_act(act_t, pre, depth, first):
        for sample in range(2):
            for layer in range(4):
                value = pre[sample, layer].reshape(128, 128).astype(F32)
                turn(act_t, sample * depth + first + layer, value)

    def transposed_edges(act_t, halo):
        for sample in range(2):
            low = halo[0, sample].reshape(128, 128).astype(F32)
            turn(act_t, sample * 6, jnp.where(slab > 0, low, 0.0))
            high = halo[1, sample].reshape(128, 128).astype(F32)
            turn(act_t, sample * 6 + 5, jnp.where(slab < 31, high, 0.0))

    def own_layers(index, carry):
        sample, layer = index // 4, lax.rem(index, 4)
        widen(x_out, sample, layer + 1, grad_out[sample, layer].reshape(128, 128).astype(F32))
        return carry

    def edges(ext, halo):
        for sample in range(2):
            low = halo[0, sample].reshape(128, 128).astype(F32)
            widen(ext, sample, 0, jnp.where(slab > 0, low, 0.0))
            high = halo[1, sample].reshape(128, 128).astype(F32)
            widen(ext, sample, 5, jnp.where(slab < 31, high, 0.0))

    def grad_by_cotangent(ext, act_t, first, depth):
        right = ext[:, 2 - depth : 6 - depth, 1:9].reshape(1024, 384)
        store_grad(first, depth, nn(act_t[...], right))

    def grad_by_act(ext, act_t, first, depth):
        out = jnp.zeros((384, 384), F32)
        for sample in range(2):
            start = (sample * 6 + depth) * 128
            out = out + nn(act_t[:, start : start + 512], ext[sample, 1:5, 1:9].reshape(512, 384))
        store_grad(first, depth, out)

    def store_grad(first, depth, out):
        for height in range(3):
            for col in range(3):
                start = first + ((depth * 3 + height) * 3 + col) * 128
                fflat[start : start + 128, :] = out[
                    height * 128 : height * 128 + 128, col * 128 : col * 128 + 128
                ]

    def back_conv(ext, weight, layers):
        acc = jnp.zeros((512, 128), F32)
        for depth in range(3):
            for height in range(3):
                rows = slice(2 - height, 10 - height)
                left = jnp.concatenate(
                    [ext[:, layer + 2 - depth, rows].reshape(256, 384) for layer in layers], axis=0
                )
                acc = acc + nt(left, weight[depth * 3 + height])
        return acc

    def place(chip):
        return {"x": lax.rem(chip // 8, 4), "y": (chip // 32) * 2 + lax.rem(chip, 2), "z": lax.rem(chip // 2, 4)}

    def unpack(chip, carry):
        where = place(chip)
        base = pl.multiple_of(chip * 216, 8)
        pieces = []
        for which in range(2):
            for part in range(3):
                value = gat[part][block(gat[part], part, [which], where)]
                pieces.append(value.astype(F32)[: VALID[part]])
        wflat[pl.ds(base, 216), :] = jnp.concatenate(pieces, axis=0)
        return carry

    def taps(weight, first, width):
        def one(index, carry):
            for col in range(3):
                start = pl.multiple_of((index * 3 + col) * width + first, 128)
                weight[index, :, col * 128 : col * 128 + 128] = wflat[pl.ds(start, width), :].astype(BF16)
            return carry

        lax.fori_loop(0, 9, one, 0)

    def pack(chip, carry):
        where = place(chip)
        base = pl.multiple_of(chip * 216, 8)
        value = fflat[pl.ds(base, 224), :]
        for which in range(2):
            for part in range(3):
                start = which * ROWS + START[part]
                rows = value[start : start + HOLD[part]].astype(BF16)
                sbs[part][block(sbs[part], part, [which], where)[1:]] = rows
        return carry

    def pack_late(chip, carry):
        where = place(chip)
        base = pl.multiple_of(chip * 216, 8)
        value = fflat[pl.ds(base, 224), :]
        value = jnp.where(core == 0, value[0:112], value[ROWS : ROWS + 112])
        for part in range(3):
            rows = value[START[part] : START[part] + HOLD[part]].astype(BF16)
            tot[part][block(tot[part], part, [], where)] = rows
        return carry

    def swap(first):
        out = []
        for part in range(3):
            group = pl.ds(first, 2)
            if part == 0:
                src, dst = sbs[0].at[other, group], rbs[0].at[group]
            else:
                src, dst = sbs[part].at[other, :, group], rbs[part].at[:, group]
            sem = (part, first // 2)
            out.append(go(copy(src, dst, swap_send.at[sem], swap_recv.at[sem], partner)))
        return out

    def core_sums(first, swapped):
        for part in range(3):
            swapped[part].wait_recv()

            def add(index, carry, part=part):
                if part == 0:
                    a, b = first + index // 4, lax.rem(index, 4)
                else:
                    a, b = index // 2, first + lax.rem(index, 2)
                total = sbs[part][core, a, b].astype(F32) + rbs[part][a, b].astype(F32)
                tot[part][EARLY, a, b] = total.astype(BF16)
                return carry

            lax.fori_loop(0, (8, 8, 4)[part], add, 0)

    def scatter(part, level, src, dst, sems):
        axis = ORDER[part][2 - level]
        out = []
        for step in (1, 3, 2):
            sem = (part, level, step - 1, sems)
            out.append(
                go(
                    copy(
                        src.at[lax.rem(at[axis] + step, 4)], dst.at[step - 1],
                        rs_send.at[sem], rs_recv.at[sem], ahead(axis, step),
                    )
                )
            )
        return out

    early_x, early_z, column = [], [], []
    for step in (1, 3, 2):
        where = moved("x", step)
        sem = (0, 0, step - 1, 0)
        c = copy(
            tot[0].at[EARLY, where["x"]], ras[0].at[EARLY, step - 1],
            rs_send.at[sem], rs_recv.at[sem], device(where, core),
        )
        early_x.append((where["x"] // 2 * 2, c))
        where = moved("y", step)
        owner = where["y"] // 2
        for number, group in enumerate((pl.ds(2, 2), pl.ds(0, 2), pl.ds(0, 4))):
            sem = (2, 0, step - 1, number)
            c = copy(
                tot[2].at[where["y"] // 2, lax.rem(where["y"], 2), group],
                ras[2].at[step - 1, group],
                rs_send.at[sem], rs_recv.at[sem], device(where, core),
            )
            column.append((number, owner, c))

    def early_sends(first):
        number = 1 - first // 2
        for owner, c in early_x:
            pl.when(owner == first)(c.start)
        group = pl.ds(first, 2)
        for step in (1, 3, 2):
            where = moved("z", step)
            sem = (1, 0, step - 1, number)
            early_z.append(
                go(
                    copy(
                        tot[1].at[EARLY, where["z"], group], ras[1].at[EARLY, step - 1, group],
                        rs_send.at[sem], rs_recv.at[sem], device(where, core),
                    )
                )
            )
        for which, owner, c in column:
            if which == number:
                pl.when(owner == EARLY)(c.start)

    def late_sends():
        out = [scatter(part, 0, tot[part].at[LATE], ras[part].at[LATE], 2) for part in range(2)]
        for which, owner, c in column:
            if which == 2:
                pl.when(owner == LATE)(c.start)
        return out

    for load in loads[1:]:
        load.wait()
    transposed_act(act_mid, pre_mid, 4, 0)
    for part in range(3):
        wait_for(leg[part])
    leg = [gather(part, 1, EARLY) for part in range(3)]
    pl.semaphore_wait(token_sem.at[0], 3)
    pl.semaphore_signal(token_sem.at[1], inc=1, device_id=ahead("y", 2), device_id_type=MESH)
    lax.fori_loop(0, 8, own_layers, 0)
    grad_by_cotangent(x_out, act_mid, FILTER, 1)
    pl.semaphore_wait(token_sem.at[1], 1)
    halos = []
    for number, (src, dst, target) in enumerate(
        (
            (grad_out.at[:, 3], halo_out.at[0], after),
            (grad_out.at[:, 0], halo_out.at[1], before),
            (pre_up.at[:, 3], halo_up.at[0], after),
            (pre_up.at[:, 0], halo_up.at[1], before),
            (coarse.at[0, :, 0], coarse.at[0, :, 2], before),
        )
    ):
        sem = 3 + number
        halos.append(go(copy(src, dst, halo_send.at[sem], halo_recv.at[sem], target)))
    third = []
    for part in (2, 0, 1):
        wait_for(leg[part])
        if part == 2:
            tall_start(EARLY)
        else:
            third.append(gather(part, 2, EARLY))
        go(core_copy(part, EARLY, 0, core))
    leg = [gather(part, 1, LATE) for part in range(2)]
    transposed_act(act_up, pre_up, 6, 1)
    wait_for(halos[0:2])
    edges(x_out, halo_out)
    grad_by_cotangent(x_out, act_mid, FILTER, 0)
    grad_by_cotangent(x_out, act_mid, FILTER, 2)
    lax.fori_loop(16, 32, pack, 0)
    two_swap = swap(2)

    def forward(part, half, copies):
        for step, c in zip((1, 3, 2), copies):
            c.wait_recv()
            go(core_copy(part, half, step, core))

    tall_forward(EARLY)
    for part in range(2):
        forward(part, EARLY, third[part])
    third = []
    for part in range(2):
        wait_for(leg[part])
        third.append(gather(part, 2, LATE))
        go(core_copy(part, LATE, 0, core))
    tall_start(LATE)
    wait_for(halos[2:])
    pair = go(copy(coarse.at[0], coarse.at[1], halo_send.at[8], halo_recv.at[8], partner))
    transposed_edges(act_up, halo_up)
    core_copy(2, EARLY, 0, other).wait_recv()
    tall_partner(EARLY)
    for part in range(2):
        wait_for([core_copy(part, EARLY, number, other) for number in range(4)])

    lax.fori_loop(16, 32, unpack, 0)
    taps(w_two, FILTER, 128)

    def mid_layers(layers):
        both = back_conv(x_out, w_two, layers)
        for number, layer in enumerate(layers):
            value = both[number * 256 : number * 256 + 256]
            keep = pre_mid[:, layer].reshape(256, 128).astype(F32) > 0.0
            value = jnp.where(keep, value, 0.0).astype(BF16)
            mid_raw[:, layer] = value.reshape(2, 8, 16, 128)

    def widen_mid(layers):
        for layer in layers:
            for sample in range(2):
                widen(x_mid, sample, layer + 1, mid_raw[sample, layer].reshape(128, 128).astype(F32))

    mid_layers((3, 0))
    mid_up = go(copy(mid_raw.at[:, 3], halo_mid.at[0], halo_send.at[0], halo_recv.at[0], after))
    mid_down = go(copy(mid_raw.at[:, 0], halo_mid.at[1], halo_send.at[1], halo_recv.at[1], before))
    core_sums(2, two_swap)
    early_sends(2)
    mid_layers((1, 2))
    widen_mid((0, 1, 2, 3))
    lax.fori_loop(0, 16, unpack, 0)
    taps(w_one, 0, 128)
    for depth in range(3):
        grad_by_act(x_mid, act_up, 0, depth)
    lax.fori_loop(0, 16, pack, 0)
    one_swap = swap(0)
    tall_forward(LATE)
    for part in range(2):
        forward(part, LATE, third[part])
    mid_up.wait_recv()
    mid_down.wait_recv()
    core_sums(0, one_swap)
    early_sends(0)
    edges(x_mid, halo_mid)

    for layers in ((3, 0), (1, 2)):
        both = back_conv(x_mid, w_one, layers)
        for number, layer in enumerate(layers):
            value = both[number * 256 : number * 256 + 256]
            keep = pre_up[:, layer].reshape(256, 128).astype(F32) > 0.0
            value = jnp.where(keep, value, 0.0).astype(BF16)
            up_raw[0, :, layer] = value.reshape(2, 128, 128)
    up_pair = go(copy(up_raw.at[0], up_raw.at[1], halo_send.at[2], halo_recv.at[2], partner))
    up_next = go(copy(up_raw.at[0, :, 3], up_before, halo_send.at[9], halo_recv.at[9], after))

    def second_sums(part, half, copies):
        wait_for(copies)
        mine = at[ORDER[part][2]]

        def add(index, carry):
            total = tot[part][half, mine, index].astype(F32)
            for step in range(3):
                total = total + ras[part][half, step, index].astype(F32)
            us[part][half, index] = total.astype(BF16)
            return carry

        lax.fori_loop(0, 4, add, 0)
        return scatter(part, 1, us[part].at[half], rcs[part].at[half], half)

    def third_sums(part, half, copies):
        wait_for(copies)
        total = us[part][half, at[ORDER[part][1]]].astype(F32)
        for step in range(3):
            total = total + rcs[part][half, step].astype(F32)
        vs[part][2 * half : 2 * half + 2] = total.astype(BF16)

    pick_row = lax.broadcasted_iota(jnp.int32, (288, 128), 0)
    pick_lane = lax.broadcasted_iota(jnp.int32, (288, 128), 1)
    tap, coarse_row, coarse_col = pick_row // 32, lax.rem(pick_row // 8, 4), lax.rem(pick_row, 8)
    fine_row = 2 * coarse_row + tap // 3 - 1
    fine_col = 2 * coarse_col + lax.rem(tap, 3) - 1
    chosen = (fine_row >= 0) & (fine_col >= 0) & (pick_lane == fine_row * 16 + fine_col)
    pick = jnp.where(chosen, 1.0, 0.0).astype(BF16)

    def spread(slot, sample, layer):
        picked = nn(pick, up_raw[slot, sample, layer]).astype(BF16)
        first = ((slot * 2 + sample) * 2 + layer // 2) * 32
        for depth in (1,) if layer % 2 == 0 else (0, 2):
            for tap in range(9):
                columns = slice((depth * 9 + tap) * 128, (depth * 9 + tap) * 128 + 128)
                gathered[first : first + 32, columns] = picked[tap * 32 : tap * 32 + 32]
        return picked

    def lower(sample, quarter, picked):
        first = (sample * 2 + quarter) * 32
        for tap in range(9):
            lowest[first : first + 32, tap * 128 : tap * 128 + 128] = picked[tap * 32 : tap * 32 + 32]

    for sample in range(2):
        for layer in range(4):
            picked = spread(0, sample, layer)
            if layer == 1:
                lower(sample, 1, picked)
    pair.wait_recv()
    turned = []
    for first in (1, 0):
        rows = []
        for slot in range(2):
            for sample in range(2):
                for quarter in (first, first + 1):
                    value = coarse[slot, sample, quarter].astype(F32)
                    if quarter == 2:
                        value = jnp.where(slab < 31, value, 0.0)
                    rows.append(value)
        turned.append(jnp.concatenate(rows, axis=0).T.astype(BF16))
    up_pair.wait_recv()
    for sample in range(2):
        for layer in range(4):
            spread(1, sample, layer)
    for index in range(9):
        out = nn(turned[min(index // 3, 1)], gathered[:, index * 384 : index * 384 + 384])
        for col in range(3):
            start = 2 * FILTER + (index * 3 + col) * 256
            fflat[start : start + 256, :] = out[:, col * 128 : col * 128 + 128]
    lax.fori_loop(32, 64, pack_late, 0)
    late_first = late_sends()
    early_first = ([c for _, c in early_x], early_z)

    tall_partner(LATE)
    for part in range(2):
        wait_for([core_copy(part, LATE, number, other) for number in range(4)])
    early_second = [second_sums(part, EARLY, early_first[part]) for part in range(2)]
    lax.fori_loop(32, 64, unpack, 0)
    taps(w_up, 2 * FILTER, 256)
    up_next.wait_recv()
    for sample in range(2):
        value = jnp.where(slab > 0, up_before[sample].astype(F32), 0.0).astype(BF16)
        lower(sample, 0, nn(pick, value).astype(BF16))
    acc = jnp.zeros((128, 256), F32)
    for index in range(9):
        if index < 3:
            left = lowest[:, index * 384 : index * 384 + 384]
        else:
            left = gathered[0:128, index * 384 : index * 384 + 384]
        acc = acc + nt(left, w_up[index])
    coarse_grad[...] = acc.astype(BF16)
    for part in range(2):
        third_sums(part, EARLY, early_second[part])

    for which, _, c in column:
        pl.when(tall_half == (LATE if which == 2 else EARLY))(c.wait_recv)
    mine = (at["y"] // 2, lax.rem(at["y"], 2))

    def add_plane(index, carry):
        total = tot[2][mine[0], mine[1], index].astype(F32)
        for step in range(3):
            total = total + ras[2][step, index].astype(F32)
        us[2][index] = total.astype(BF16)
        return carry

    lax.fori_loop(0, 4, add_plane, 0)
    plane = scatter(2, 1, us[2], rcs[2], 0)
    late_second = [second_sums(part, LATE, late_first[part]) for part in range(2)]
    wait_for(plane)
    total = us[2][at["x"]].astype(F32)
    for step in range(3):
        total = total + rcs[2][step].astype(F32)
    vs[2][...] = total.astype(BF16)
    last = [None, None, scatter(2, 2, vs[2], rds[2], 0)]
    for part in range(2):
        third_sums(part, LATE, late_second[part])
        last[part] = scatter(part, 2, vs[part], rds[part], 0)
    for part in (2, 0, 1):
        wait_for(last[part])
        total = vs[part][at[ORDER[part][0]]].astype(F32)
        for step in range(3):
            total = total + rds[part][step].astype(F32)
        summed[START[part] : START[part] + VALID[part], :] = total[: VALID[part]]
    for c in started:
        c.wait_send()
    for _, c in early_x:
        c.wait_send()
    for which, owner, c in column:
        pl.when(owner == (LATE if which == 2 else EARLY))(c.wait_send)
    for step, _, c, _ in tall:
        c.wait_send()
        core_copy(2, 0, step, core).wait_send()


def finish(coarse, summed, master, moment, second, coarse_grad, new_master, new_moment, new_second):
    coarse_grad[...] = coarse[...].astype(F32).reshape(coarse_grad.shape).astype(BF16)
    mean_grad = summed[...] / 8.0
    first = beta_one * moment[...] + (1.0 - beta_one) * mean_grad
    squared = beta_two * second[...] + (1.0 - beta_two) * mean_grad * mean_grad
    corrected = first / (1.0 - beta_one**adam_step)
    scaled = jnp.sqrt(squared / (1.0 - beta_two**adam_step)) + adam_eps
    new_moment[...] = first
    new_second[...] = squared
    new_master[...] = master[...] - learn_rate * corrected / scaled


def body(coarse_in, pre_up, pre_mid, grad_out, master, moment, second):
    vmem = pl.BlockSpec(memory_space=pltpu.VMEM)
    held = pl.BlockSpec(memory_space=pl.ANY)
    scratch = [
        pltpu.VMEM((ROWS, 128), F32),
        pltpu.VMEM((2, 4, 8, 16, 128), BF16),
        pltpu.VMEM((2, 4, 8, 16, 128), BF16),
        pltpu.VMEM((2, 4, 8, 16, 128), BF16),
        pltpu.VMEM((2, 2, 3, 32, 256), BF16),
    ]
    for shape, column in (
        ((2, 2, 4, 4, 2), (2, 2, 2, 4, 4)),
        ((2, 4, 4, 2), (2, 2, 4, 4)),
        ((4, 4, 2), (2, 4, 4)),
        ((2, 4, 4, 2), (2, 2, 4, 4)),
        ((2, 3, 4, 2), (3, 4, 4)),
        ((2, 4, 2), (4, 4)),
        ((2, 3, 2), (3, 4)),
        ((4,), (4,)),
        ((3,), (3,)),
    ):
        for part in range(3):
            lead = column if part == 2 else shape
            scratch.append(pltpu.VMEM(lead + (HOLD[part], 128), BF16))
    scratch += [
        pltpu.VMEM((TOTAL, 128), F32),
        pltpu.VMEM((TOTAL + 8, 128), F32),
        pltpu.VMEM((9, 128, 384), BF16),
        pltpu.VMEM((9, 128, 384), BF16),
        pltpu.VMEM((9, 256, 384), BF16),
        pltpu.VMEM((2, 6, 10, 16, 384), BF16),
        pltpu.VMEM((2, 6, 10, 16, 384), BF16),
        pltpu.VMEM((384, 1024), BF16),
        pltpu.VMEM((384, 1536), BF16),
        pltpu.VMEM((2, 4, 8, 16, 128), BF16),
        pltpu.VMEM((2, 2, 4, 128, 128), BF16),
        pltpu.VMEM((2, 128, 128), BF16),
        pltpu.VMEM((256, FILTER), BF16),
        pltpu.VMEM((128, 9 * 128), BF16),
        pltpu.VMEM((2, 2, 8, 16, 128), BF16),
        pltpu.VMEM((2, 2, 8, 16, 128), BF16),
        pltpu.VMEM((2, 2, 8, 16, 128), BF16),
    ]
    for shape in ((3, 3, 3, 2), (3, 2, 4), (3, 3, 3, 3), (3, 2), (10,)):
        scratch += [pltpu.SemaphoreType.DMA(shape)] * 2
    scratch += [pltpu.SemaphoreType.DMA((5,)), pltpu.SemaphoreType.REGULAR((2,))]
    coarse_grad, summed = pl.pallas_call(
        kernel,
        out_shape=(
            jax.ShapeDtypeStruct((128, 256), BF16),
            jax.ShapeDtypeStruct((ROWS, 128), F32),
        ),
        in_specs=[held] * 5,
        out_specs=(vmem, vmem),
        scratch_shapes=scratch,
        compiler_params=pltpu.CompilerParams(
            collective_id=0, has_side_effects=True, vmem_limit_bytes=56 * 1024 * 1024
        ),
    )(
        master,
        grad_out.reshape(grad_out.shape[1:]),
        pre_mid.reshape(pre_mid.shape[1:]),
        pre_up.reshape(pre_up.shape[1:]),
        coarse_in.reshape(2, 2, 32, 256),
    )
    coarse_shape = jax.ShapeDtypeStruct(coarse_in.shape, BF16)
    rows_shape = jax.ShapeDtypeStruct((ROWS, 128), F32)
    return tuple(
        pl.pallas_call(
            finish,
            out_shape=(coarse_shape, rows_shape, rows_shape, rows_shape),
            in_specs=[vmem] * 5,
            out_specs=(vmem,) * 4,
        )(coarse_grad, summed, master, moment, second)
    )


def solution(mesh):
    wide = P("dp", None, "slab", None, None, None)
    flat = P(("slab", "dp"), None)
    return jax.shard_map(
        body,
        mesh=mesh,
        in_specs=(wide, wide, wide, wide, flat, flat, flat),
        out_specs=(wide, flat, flat, flat),
        check_vma=False,
    )
```

```python
import jax
import jax.numpy as jnp
from jax import lax
from jax.experimental import pallas as pl
from jax.experimental.pallas import tpu as pltpu
from jax.sharding import PartitionSpec as P

beta_one = 0.9
beta_two = 0.999
adam_step = 10.0
learn_rate = 0.01
adam_eps = 1e-08

F32 = jnp.float32
BF16 = jnp.bfloat16
MESH = pl.DeviceIdType.MESH

ROWS = 108
TOTAL = 13824
FILTER = 3456
START = (0, 48, 80)
HOLD = (48, 32, 32)
VALID = (48, 32, 28)
ORDER = (("y", "z", "x"), ("y", "x", "z"), ("z", "x", "y"))
EARLY, LATE = 0, 1


def nt(left, right):
    return lax.dot_general(
        left, right, (((1,), (1,)), ((), ())), preferred_element_type=F32
    )


def nn(left, right):
    return jnp.dot(left, right, preferred_element_type=F32)


def kernel(
    master_in, grad_out_in, pre_mid_in, pre_up_in, coarse_in,
    coarse_grad, summed,
    master, grad_out, pre_mid, pre_up, coarse,
    g0, g1, g2, sb0, sb1, sb2, rb0, rb1, rb2, t0, t1, t2, ra0, ra1, ra2,
    u0, u1, u2, rc0, rc1, rc2, v0, v1, v2, rd0, rd1, rd2,
    wflat, fflat, w_one, w_two, w_up, x_out, x_mid, act_mid, act_up, mid_raw, up_raw, up_before,
    gathered, lowest, halo_out, halo_mid, halo_up,
    ag_send, ag_recv, core_send, core_recv, rs_send, rs_recv, swap_send, swap_recv,
    halo_send, halo_recv, load_sem, token_sem,
):
    gat, sbs, rbs, tot = (g0, g1, g2), (sb0, sb1, sb2), (rb0, rb1, rb2), (t0, t1, t2)
    ras, us, rcs, vs, rds = (
        (ra0, ra1, ra2), (u0, u1, u2), (rc0, rc1, rc2), (v0, v1, v2), (rd0, rd1, rd2),
    )
    slab, dp = lax.axis_index("slab"), lax.axis_index("dp")
    at = {
        "x": lax.rem(slab // 4, 4),
        "y": (slab // 16) * 2 + dp // 2,
        "z": lax.rem(slab, 4),
    }
    core = lax.rem(dp, 2)
    other = 1 - core

    def device(where, which):
        return (
            (where["y"] // 2) * 16 + where["x"] * 4 + where["z"],
            lax.rem(where["y"], 2) * 2 + which,
        )

    def moved(axis, step):
        where = dict(at)
        where[axis] = lax.rem(at[axis] + step, 4)
        return where

    def ahead(axis, step):
        return device(moved(axis, step), core)

    partner = device(at, other)
    after = (lax.rem(slab + 1, 32), dp)
    before = (lax.rem(slab + 31, 32), dp)

    def copy(src, dst, send, recv, target):
        return pltpu.make_async_remote_copy(
            src_ref=src, dst_ref=dst, send_sem=send, recv_sem=recv,
            device_id=target, device_id_type=MESH,
        )

    barrier = pltpu.get_barrier_semaphore()
    targets = [partner]
    targets += [ahead(axis, step) for axis in ("x", "y", "z") for step in (1, 2, 3)]
    for target in targets:
        pl.semaphore_signal(barrier, inc=1, device_id=target, device_id_type=MESH)

    def block(ref, part, lead, where):
        axes = ORDER[part]
        if part == 2:
            inner = [lax.rem(where["y"], 2), where["x"], where["z"]]
        else:
            inner = [where[axes[2]], where[axes[1]], lax.rem(where["y"], 2)]
        return tuple([where["y"] // 2] + lead + inner)

    loads = [
        pltpu.make_async_copy(src, dst, load_sem.at[number])
        for number, (src, dst) in enumerate(
            (
                (master_in, master),
                (grad_out_in, grad_out),
                (pre_mid_in, pre_mid),
                (pre_up_in, pre_up),
                (coarse_in, coarse.at[0, :, 0:2]),
            )
        )
    ]
    for load in loads:
        load.start()

    loads[0].wait()
    for part in range(3):
        rows = master[START[part] : START[part] + VALID[part], :]
        if HOLD[part] > VALID[part]:
            rows = jnp.concatenate(
                [rows, jnp.zeros((HOLD[part] - VALID[part], 128), F32)], axis=0
            )
        gat[part][block(gat[part], part, [core], at)] = rows.astype(BF16)
    pl.semaphore_wait(barrier, len(targets))

    started = []

    def go(c):
        c.start()
        started.append(c)
        return c

    def piece(part, which, level, half, where):
        place = block(gat[part], part, [which], where)
        if part == 2:
            return gat[part].at[place[: 5 - level]]
        if level == 0:
            return gat[part].at[place]
        return gat[part].at[(half,) + place[1 : 5 - level]]

    def back_half(step):
        return lax.rem(at["y"] + 4 - step, 4) // 2

    def gather(part, level, half):
        axis = ORDER[part][level]
        out = []
        for step in (1, 3, 2):
            sem = (part, level, step - 1, half)
            src = piece(part, core, level, half, at)
            go(copy(src, src, ag_send.at[sem], ag_recv.at[sem], ahead(axis, step)))
            dst = piece(part, core, level, half, moved(axis, 4 - step))
            out.append(copy(dst, dst, ag_send.at[sem], ag_recv.at[sem], partner))
        return out

    tall_half = at["y"] // 2
    tall = []
    for step in (1, 3, 2):
        sem = (2, 2, step - 1, 0)
        src = piece(2, core, 2, 0, at)
        dst = piece(2, core, 2, 0, moved("y", 4 - step))
        tall.append(
            (
                step,
                back_half(step),
                copy(src, src, ag_send.at[sem], ag_recv.at[sem], ahead("y", step)),
                copy(dst, dst, ag_send.at[sem], ag_recv.at[sem], partner),
            )
        )

    def tall_start(half):
        for _, _, c, _ in tall:
            pl.when(tall_half == half)(c.start)

    def tall_forward(half):
        for step, owner, _, c in tall:

            @pl.when(owner == half)
            def _():
                c.wait_recv()
                core_copy(2, 0, step, core).start()

    def tall_partner(half):
        for step, owner, _, _ in tall:
            pl.when(owner == half)(core_copy(2, 0, step, other).wait_recv)

    def core_copy(part, half, number, which):
        axis = ORDER[part][2]
        ref = piece(part, which, 2, half, moved(axis, 4 - number))
        sem = (part, half, number)
        return copy(ref, ref, core_send.at[sem], core_recv.at[sem], partner)

    def wait_for(copies):
        for c in copies:
            c.wait_recv()

    leg = [gather(part, 0, EARLY) for part in range(3)]
    for step in (1, 3, 2):
        pl.semaphore_signal(token_sem.at[0], inc=1, device_id=ahead("z", step), device_id_type=MESH)

    row = lax.broadcasted_iota(jnp.int32, (128, 128), 0)
    lane = lax.broadcasted_iota(jnp.int32, (128, 128), 1)
    breadth = lax.rem(row, 16)
    for ext in (x_out, x_mid):
        ext[:, :, 0] = jnp.zeros((2, 6, 16, 384), BF16)
        ext[:, :, 9] = jnp.zeros((2, 6, 16, 384), BF16)
    fflat[TOTAL : TOTAL + 8, :] = jnp.zeros((8, 128), F32)

    def widen(ext, sample, layer, value):
        later = jnp.where(breadth == 15, 0.0, pltpu.roll(value, 127, 0))
        earlier = jnp.where(breadth == 0, 0.0, pltpu.roll(value, 1, 0))
        wide = jnp.concatenate(
            [later.astype(BF16), value.astype(BF16), earlier.astype(BF16)], axis=1
        )
        ext[sample, layer, 1:9] = wide.reshape(8, 16, 384)

    def turn(act_t, first, value):
        turned = jnp.maximum(value, 0.0).T
        columns = slice(first * 128, first * 128 + 128)
        low = jnp.where(lane < 16, 0.0, pltpu.roll(turned, 16, 1))
        high = jnp.where(lane >= 112, 0.0, pltpu.roll(turned, 112, 1))
        act_t[0:128, columns] = low.astype(BF16)
        act_t[128:256, columns] = turned.astype(BF16)
        act_t[256:384, columns] = high.astype(BF16)

    def transposed_act(act_t, pre, depth, first):
        for sample in range(2):
            for layer in range(4):
                value = pre[sample, layer].reshape(128, 128).astype(F32)
                turn(act_t, sample * depth + first + layer, value)

    def transposed_edges(act_t, halo):
        for sample in range(2):
            low = halo[0, sample].reshape(128, 128).astype(F32)
            turn(act_t, sample * 6, jnp.where(slab > 0, low, 0.0))
            high = halo[1, sample].reshape(128, 128).astype(F32)
            turn(act_t, sample * 6 + 5, jnp.where(slab < 31, high, 0.0))

    def own_layers(index, carry):
        sample, layer = index // 4, lax.rem(index, 4)
        widen(x_out, sample, layer + 1, grad_out[sample, layer].reshape(128, 128).astype(F32))
        return carry

    def edges(ext, halo):
        for sample in range(2):
            low = halo[0, sample].reshape(128, 128).astype(F32)
            widen(ext, sample, 0, jnp.where(slab > 0, low, 0.0))
            high = halo[1, sample].reshape(128, 128).astype(F32)
            widen(ext, sample, 5, jnp.where(slab < 31, high, 0.0))

    def grad_by_cotangent(ext, act_t, first, depth):
        right = ext[:, 2 - depth : 6 - depth, 1:9].reshape(1024, 384)
        store_grad(first, depth, nn(act_t[...], right))

    def grad_by_act(ext, act_t, first, depth):
        out = jnp.zeros((384, 384), F32)
        for sample in range(2):
            start = (sample * 6 + depth) * 128
            out = out + nn(act_t[:, start : start + 512], ext[sample, 1:5, 1:9].reshape(512, 384))
        store_grad(first, depth, out)

    def store_grad(first, depth, out):
        for height in range(3):
            for col in range(3):
                start = first + ((depth * 3 + height) * 3 + col) * 128
                fflat[start : start + 128, :] = out[
                    height * 128 : height * 128 + 128, col * 128 : col * 128 + 128
                ]

    def back_conv(ext, weight, layers):
        acc = jnp.zeros((512, 128), F32)
        for depth in range(3):
            for height in range(3):
                rows = slice(2 - height, 10 - height)
                left = jnp.concatenate(
                    [ext[:, layer + 2 - depth, rows].reshape(256, 384) for layer in layers], axis=0
                )
                acc = acc + nt(left, weight[depth * 3 + height])
        return acc

    def place(chip):
        return {"x": lax.rem(chip // 8, 4), "y": (chip // 32) * 2 + lax.rem(chip, 2), "z": lax.rem(chip // 2, 4)}

    def unpack(chip, carry):
        where = place(chip)
        base = pl.multiple_of(chip * 216, 8)
        pieces = []
        for which in range(2):
            for part in range(3):
                value = gat[part][block(gat[part], part, [which], where)]
                pieces.append(value.astype(F32)[: VALID[part]])
        wflat[pl.ds(base, 216), :] = jnp.concatenate(pieces, axis=0)
        return carry

    def taps(weight, first, width):
        def one(index, carry):
            for col in range(3):
                start = pl.multiple_of((index * 3 + col) * width + first, 128)
                weight[index, :, col * 128 : col * 128 + 128] = wflat[pl.ds(start, width), :].astype(BF16)
            return carry

        lax.fori_loop(0, 9, one, 0)

    def pack(chip, carry):
        where = place(chip)
        base = pl.multiple_of(chip * 216, 8)
        value = fflat[pl.ds(base, 224), :]
        for which in range(2):
            for part in range(3):
                start = which * ROWS + START[part]
                rows = value[start : start + HOLD[part]].astype(BF16)
                sbs[part][block(sbs[part], part, [which], where)[1:]] = rows
        return carry

    def pack_late(chip, carry):
        where = place(chip)
        base = pl.multiple_of(chip * 216, 8)
        value = fflat[pl.ds(base, 224), :]
        value = jnp.where(core == 0, value[0:112], value[ROWS : ROWS + 112])
        for part in range(3):
            rows = value[START[part] : START[part] + HOLD[part]].astype(BF16)
            tot[part][block(tot[part], part, [], where)] = rows
        return carry

    def swap(first):
        out = []
        for part in range(3):
            group = pl.ds(first, 2)
            if part == 0:
                src, dst = sbs[0].at[other, group], rbs[0].at[group]
            else:
                src, dst = sbs[part].at[other, :, group], rbs[part].at[:, group]
            sem = (part, first // 2)
            out.append(go(copy(src, dst, swap_send.at[sem], swap_recv.at[sem], partner)))
        return out

    def core_sums(first, swapped):
        for part in range(3):
            swapped[part].wait_recv()

            def add(index, carry, part=part):
                if part == 0:
                    a, b = first + index // 4, lax.rem(index, 4)
                else:
                    a, b = index // 2, first + lax.rem(index, 2)
                total = sbs[part][core, a, b].astype(F32) + rbs[part][a, b].astype(F32)
                tot[part][EARLY, a, b] = total.astype(BF16)
                return carry

            lax.fori_loop(0, (8, 8, 4)[part], add, 0)

    def scatter(part, level, src, dst, sems):
        axis = ORDER[part][2 - level]
        out = []
        for step in (1, 3, 2):
            sem = (part, level, step - 1, sems)
            out.append(
                go(
                    copy(
                        src.at[lax.rem(at[axis] + step, 4)], dst.at[step - 1],
                        rs_send.at[sem], rs_recv.at[sem], ahead(axis, step),
                    )
                )
            )
        return out

    early_x, early_z, column = [], [], []
    for step in (1, 3, 2):
        where = moved("x", step)
        sem = (0, 0, step - 1, 0)
        c = copy(
            tot[0].at[EARLY, where["x"]], ras[0].at[EARLY, step - 1],
            rs_send.at[sem], rs_recv.at[sem], device(where, core),
        )
        early_x.append((where["x"] // 2 * 2, c))
        where = moved("y", step)
        owner = where["y"] // 2
        for number, group in enumerate((pl.ds(2, 2), pl.ds(0, 2), pl.ds(0, 4))):
            sem = (2, 0, step - 1, number)
            c = copy(
                tot[2].at[where["y"] // 2, lax.rem(where["y"], 2), group],
                ras[2].at[step - 1, group],
                rs_send.at[sem], rs_recv.at[sem], device(where, core),
            )
            column.append((number, owner, c))

    def early_sends(first):
        number = 1 - first // 2
        for owner, c in early_x:
            pl.when(owner == first)(c.start)
        group = pl.ds(first, 2)
        for step in (1, 3, 2):
            where = moved("z", step)
            sem = (1, 0, step - 1, number)
            early_z.append(
                go(
                    copy(
                        tot[1].at[EARLY, where["z"], group], ras[1].at[EARLY, step - 1, group],
                        rs_send.at[sem], rs_recv.at[sem], device(where, core),
                    )
                )
            )
        for which, owner, c in column:
            if which == number:
                pl.when(owner == EARLY)(c.start)

    def late_sends():
        out = [scatter(part, 0, tot[part].at[LATE], ras[part].at[LATE], 2) for part in range(2)]
        for which, owner, c in column:
            if which == 2:
                pl.when(owner == LATE)(c.start)
        return out

    for load in loads[1:]:
        load.wait()
    transposed_act(act_mid, pre_mid, 4, 0)
    for part in range(3):
        wait_for(leg[part])
    leg = [gather(part, 1, EARLY) for part in range(3)]
    pl.semaphore_wait(token_sem.at[0], 3)
    pl.semaphore_signal(token_sem.at[1], inc=1, device_id=ahead("y", 2), device_id_type=MESH)
    lax.fori_loop(0, 8, own_layers, 0)
    grad_by_cotangent(x_out, act_mid, FILTER, 1)
    pl.semaphore_wait(token_sem.at[1], 1)
    halos = []
    for number, (src, dst, target) in enumerate(
        (
            (grad_out.at[:, 3], halo_out.at[0], after),
            (grad_out.at[:, 0], halo_out.at[1], before),
            (pre_up.at[:, 3], halo_up.at[0], after),
            (pre_up.at[:, 0], halo_up.at[1], before),
            (coarse.at[0, :, 0], coarse.at[0, :, 2], before),
        )
    ):
        sem = 3 + number
        halos.append(go(copy(src, dst, halo_send.at[sem], halo_recv.at[sem], target)))
    third = []
    for part in (2, 0, 1):
        wait_for(leg[part])
        if part == 2:
            tall_start(EARLY)
        else:
            third.append(gather(part, 2, EARLY))
        go(core_copy(part, EARLY, 0, core))
    leg = [gather(part, 1, LATE) for part in range(2)]
    transposed_act(act_up, pre_up, 6, 1)
    wait_for(halos[0:2])
    edges(x_out, halo_out)
    grad_by_cotangent(x_out, act_mid, FILTER, 0)
    grad_by_cotangent(x_out, act_mid, FILTER, 2)
    lax.fori_loop(16, 32, pack, 0)
    two_swap = swap(2)

    def forward(part, half, copies):
        for step, c in zip((1, 3, 2), copies):
            c.wait_recv()
            go(core_copy(part, half, step, core))

    tall_forward(EARLY)
    for part in range(2):
        forward(part, EARLY, third[part])
    third = []
    for part in range(2):
        wait_for(leg[part])
        third.append(gather(part, 2, LATE))
        go(core_copy(part, LATE, 0, core))
    tall_start(LATE)
    wait_for(halos[2:])
    pair = go(copy(coarse.at[0], coarse.at[1], halo_send.at[8], halo_recv.at[8], partner))
    transposed_edges(act_up, halo_up)
    core_copy(2, EARLY, 0, other).wait_recv()
    tall_partner(EARLY)
    for part in range(2):
        wait_for([core_copy(part, EARLY, number, other) for number in range(4)])

    lax.fori_loop(16, 32, unpack, 0)
    taps(w_two, FILTER, 128)

    def mid_layers(layers):
        both = back_conv(x_out, w_two, layers)
        for number, layer in enumerate(layers):
            value = both[number * 256 : number * 256 + 256]
            keep = pre_mid[:, layer].reshape(256, 128).astype(F32) > 0.0
            value = jnp.where(keep, value, 0.0).astype(BF16)
            mid_raw[:, layer] = value.reshape(2, 8, 16, 128)

    def widen_mid(layers):
        for layer in layers:
            for sample in range(2):
                widen(x_mid, sample, layer + 1, mid_raw[sample, layer].reshape(128, 128).astype(F32))

    mid_layers((3, 0))
    mid_up = go(copy(mid_raw.at[:, 3], halo_mid.at[0], halo_send.at[0], halo_recv.at[0], after))
    mid_down = go(copy(mid_raw.at[:, 0], halo_mid.at[1], halo_send.at[1], halo_recv.at[1], before))
    core_sums(2, two_swap)
    early_sends(2)
    mid_layers((1, 2))
    widen_mid((0, 1, 2, 3))
    for depth in range(3):
        grad_by_act(x_mid, act_up, 0, depth)
    lax.fori_loop(0, 16, pack, 0)
    one_swap = swap(0)
    lax.fori_loop(0, 16, unpack, 0)
    taps(w_one, 0, 128)
    core_sums(0, one_swap)
    early_sends(0)
    tall_forward(LATE)
    for part in range(2):
        forward(part, LATE, third[part])
    mid_up.wait_recv()
    mid_down.wait_recv()
    edges(x_mid, halo_mid)

    for layers in ((3, 0), (1, 2)):
        both = back_conv(x_mid, w_one, layers)
        for number, layer in enumerate(layers):
            value = both[number * 256 : number * 256 + 256]
            keep = pre_up[:, layer].reshape(256, 128).astype(F32) > 0.0
            value = jnp.where(keep, value, 0.0).astype(BF16)
            up_raw[0, :, layer] = value.reshape(2, 128, 128)
    up_pair = go(copy(up_raw.at[0], up_raw.at[1], halo_send.at[2], halo_recv.at[2], partner))
    up_next = go(copy(up_raw.at[0, :, 3], up_before, halo_send.at[9], halo_recv.at[9], after))

    def second_sums(part, half, copies):
        wait_for(copies)
        mine = at[ORDER[part][2]]

        def add(index, carry):
            total = tot[part][half, mine, index].astype(F32)
            for step in range(3):
                total = total + ras[part][half, step, index].astype(F32)
            us[part][half, index] = total.astype(BF16)
            return carry

        lax.fori_loop(0, 4, add, 0)
        return scatter(part, 1, us[part].at[half], rcs[part].at[half], half)

    def third_sums(part, half, copies):
        wait_for(copies)
        total = us[part][half, at[ORDER[part][1]]].astype(F32)
        for step in range(3):
            total = total + rcs[part][half, step].astype(F32)
        vs[part][2 * half : 2 * half + 2] = total.astype(BF16)

    pick_row = lax.broadcasted_iota(jnp.int32, (288, 128), 0)
    pick_lane = lax.broadcasted_iota(jnp.int32, (288, 128), 1)
    tap, coarse_row, coarse_col = pick_row // 32, lax.rem(pick_row // 8, 4), lax.rem(pick_row, 8)
    fine_row = 2 * coarse_row + tap // 3 - 1
    fine_col = 2 * coarse_col + lax.rem(tap, 3) - 1
    chosen = (fine_row >= 0) & (fine_col >= 0) & (pick_lane == fine_row * 16 + fine_col)
    pick = jnp.where(chosen, 1.0, 0.0).astype(BF16)

    def spread(slot, sample, layer):
        picked = nn(pick, up_raw[slot, sample, layer]).astype(BF16)
        first = ((slot * 2 + sample) * 2 + layer // 2) * 32
        for depth in (1,) if layer % 2 == 0 else (0, 2):
            for tap in range(9):
                columns = slice((depth * 9 + tap) * 128, (depth * 9 + tap) * 128 + 128)
                gathered[first : first + 32, columns] = picked[tap * 32 : tap * 32 + 32]
        return picked

    def lower(sample, quarter, picked):
        first = (sample * 2 + quarter) * 32
        for tap in range(9):
            lowest[first : first + 32, tap * 128 : tap * 128 + 128] = picked[tap * 32 : tap * 32 + 32]

    for sample in range(2):
        for layer in range(4):
            picked = spread(0, sample, layer)
            if layer == 1:
                lower(sample, 1, picked)
    pair.wait_recv()
    turned = []
    for first in (1, 0):
        rows = []
        for slot in range(2):
            for sample in range(2):
                for quarter in (first, first + 1):
                    value = coarse[slot, sample, quarter].astype(F32)
                    if quarter == 2:
                        value = jnp.where(slab < 31, value, 0.0)
                    rows.append(value)
        turned.append(jnp.concatenate(rows, axis=0).T.astype(BF16))
    up_pair.wait_recv()
    for sample in range(2):
        for layer in range(4):
            spread(1, sample, layer)
    for index in range(9):
        out = nn(turned[min(index // 3, 1)], gathered[:, index * 384 : index * 384 + 384])
        for col in range(3):
            start = 2 * FILTER + (index * 3 + col) * 256
            fflat[start : start + 256, :] = out[:, col * 128 : col * 128 + 128]
    lax.fori_loop(32, 64, pack_late, 0)
    late_first = late_sends()
    early_first = ([c for _, c in early_x], early_z)

    tall_partner(LATE)
    for part in range(2):
        wait_for([core_copy(part, LATE, number, other) for number in range(4)])
    lax.fori_loop(32, 64, unpack, 0)
    taps(w_up, 2 * FILTER, 256)
    up_next.wait_recv()
    for sample in range(2):
        value = jnp.where(slab > 0, up_before[sample].astype(F32), 0.0).astype(BF16)
        lower(sample, 0, nn(pick, value).astype(BF16))
    acc = jnp.zeros((128, 256), F32)
    for index in range(9):
        if index < 3:
            left = lowest[:, index * 384 : index * 384 + 384]
        else:
            left = gathered[0:128, index * 384 : index * 384 + 384]
        acc = acc + nt(left, w_up[index])
    coarse_grad[...] = acc.astype(BF16)
    early_second = [second_sums(part, EARLY, early_first[part]) for part in range(2)]

    for which, _, c in column:
        pl.when(tall_half == (LATE if which == 2 else EARLY))(c.wait_recv)
    mine = (at["y"] // 2, lax.rem(at["y"], 2))

    def add_plane(index, carry):
        total = tot[2][mine[0], mine[1], index].astype(F32)
        for step in range(3):
            total = total + ras[2][step, index].astype(F32)
        us[2][index] = total.astype(BF16)
        return carry

    lax.fori_loop(0, 4, add_plane, 0)
    plane = scatter(2, 1, us[2], rcs[2], 0)
    late_second = [second_sums(part, LATE, late_first[part]) for part in range(2)]
    for part in range(2):
        third_sums(part, EARLY, early_second[part])
    wait_for(plane)
    total = us[2][at["x"]].astype(F32)
    for step in range(3):
        total = total + rcs[2][step].astype(F32)
    vs[2][...] = total.astype(BF16)
    last = [None, None, scatter(2, 2, vs[2], rds[2], 0)]
    for part in range(2):
        third_sums(part, LATE, late_second[part])
        last[part] = scatter(part, 2, vs[part], rds[part], 0)
    for part in (2, 0, 1):
        wait_for(last[part])
        total = vs[part][at[ORDER[part][0]]].astype(F32)
        for step in range(3):
            total = total + rds[part][step].astype(F32)
        summed[START[part] : START[part] + VALID[part], :] = total[: VALID[part]]
    for c in started:
        c.wait_send()
    for _, c in early_x:
        c.wait_send()
    for which, owner, c in column:
        pl.when(owner == (LATE if which == 2 else EARLY))(c.wait_send)
    for step, _, c, _ in tall:
        c.wait_send()
        core_copy(2, 0, step, core).wait_send()


def finish(coarse, summed, master, moment, second, coarse_grad, new_master, new_moment, new_second):
    coarse_grad[...] = coarse[...].astype(F32).reshape(coarse_grad.shape).astype(BF16)
    mean_grad = summed[...] / 8.0
    first = beta_one * moment[...] + (1.0 - beta_one) * mean_grad
    squared = beta_two * second[...] + (1.0 - beta_two) * mean_grad * mean_grad
    corrected = first / (1.0 - beta_one**adam_step)
    scaled = jnp.sqrt(squared / (1.0 - beta_two**adam_step)) + adam_eps
    new_moment[...] = first
    new_second[...] = squared
    new_master[...] = master[...] - learn_rate * corrected / scaled


def body(coarse_in, pre_up, pre_mid, grad_out, master, moment, second):
    vmem = pl.BlockSpec(memory_space=pltpu.VMEM)
    held = pl.BlockSpec(memory_space=pl.ANY)
    scratch = [
        pltpu.VMEM((ROWS, 128), F32),
        pltpu.VMEM((2, 4, 8, 16, 128), BF16),
        pltpu.VMEM((2, 4, 8, 16, 128), BF16),
        pltpu.VMEM((2, 4, 8, 16, 128), BF16),
        pltpu.VMEM((2, 2, 3, 32, 256), BF16),
    ]
    for shape, column in (
        ((2, 2, 4, 4, 2), (2, 2, 2, 4, 4)),
        ((2, 4, 4, 2), (2, 2, 4, 4)),
        ((4, 4, 2), (2, 4, 4)),
        ((2, 4, 4, 2), (2, 2, 4, 4)),
        ((2, 3, 4, 2), (3, 4, 4)),
        ((2, 4, 2), (4, 4)),
        ((2, 3, 2), (3, 4)),
        ((4,), (4,)),
        ((3,), (3,)),
    ):
        for part in range(3):
            lead = column if part == 2 else shape
            scratch.append(pltpu.VMEM(lead + (HOLD[part], 128), BF16))
    scratch += [
        pltpu.VMEM((TOTAL, 128), F32),
        pltpu.VMEM((TOTAL + 8, 128), F32),
        pltpu.VMEM((9, 128, 384), BF16),
        pltpu.VMEM((9, 128, 384), BF16),
        pltpu.VMEM((9, 256, 384), BF16),
        pltpu.VMEM((2, 6, 10, 16, 384), BF16),
        pltpu.VMEM((2, 6, 10, 16, 384), BF16),
        pltpu.VMEM((384, 1024), BF16),
        pltpu.VMEM((384, 1536), BF16),
        pltpu.VMEM((2, 4, 8, 16, 128), BF16),
        pltpu.VMEM((2, 2, 4, 128, 128), BF16),
        pltpu.VMEM((2, 128, 128), BF16),
        pltpu.VMEM((256, FILTER), BF16),
        pltpu.VMEM((128, 9 * 128), BF16),
        pltpu.VMEM((2, 2, 8, 16, 128), BF16),
        pltpu.VMEM((2, 2, 8, 16, 128), BF16),
        pltpu.VMEM((2, 2, 8, 16, 128), BF16),
    ]
    for shape in ((3, 3, 3, 2), (3, 2, 4), (3, 3, 3, 3), (3, 2), (10,)):
        scratch += [pltpu.SemaphoreType.DMA(shape)] * 2
    scratch += [pltpu.SemaphoreType.DMA((5,)), pltpu.SemaphoreType.REGULAR((2,))]
    coarse_grad, summed = pl.pallas_call(
        kernel,
        out_shape=(
            jax.ShapeDtypeStruct((128, 256), BF16),
            jax.ShapeDtypeStruct((ROWS, 128), F32),
        ),
        in_specs=[held] * 5,
        out_specs=(vmem, vmem),
        scratch_shapes=scratch,
        compiler_params=pltpu.CompilerParams(
            collective_id=0, has_side_effects=True, vmem_limit_bytes=56 * 1024 * 1024
        ),
    )(
        master,
        grad_out.reshape(grad_out.shape[1:]),
        pre_mid.reshape(pre_mid.shape[1:]),
        pre_up.reshape(pre_up.shape[1:]),
        coarse_in.reshape(2, 2, 32, 256),
    )
    coarse_shape = jax.ShapeDtypeStruct(coarse_in.shape, BF16)
    rows_shape = jax.ShapeDtypeStruct((ROWS, 128), F32)
    return tuple(
        pl.pallas_call(
            finish,
            out_shape=(coarse_shape, rows_shape, rows_shape, rows_shape),
            in_specs=[vmem] * 5,
            out_specs=(vmem,) * 4,
        )(coarse_grad, summed, master, moment, second)
    )


def solution(mesh):
    wide = P("dp", None, "slab", None, None, None)
    flat = P(("slab", "dp"), None)
    return jax.shard_map(
        body,
        mesh=mesh,
        in_specs=(wide, wide, wide, wide, flat, flat, flat),
        out_specs=(wide, flat, flat, flat),
        check_vma=False,
    )
```

```python
import jax
import jax.numpy as jnp
from jax import lax
from jax.experimental import pallas as pl
from jax.experimental.pallas import tpu as pltpu
from jax.sharding import PartitionSpec as P

beta_one = 0.9
beta_two = 0.999
adam_step = 10.0
learn_rate = 0.01
adam_eps = 1e-08

F32 = jnp.float32
BF16 = jnp.bfloat16
MESH = pl.DeviceIdType.MESH

ROWS = 108
TOTAL = 13824
FILTER = 3456
START = (0, 48, 80)
HOLD = (48, 32, 32)
VALID = (48, 32, 28)
ORDER = (("y", "z", "x"), ("y", "x", "z"), ("z", "x", "y"))
EARLY, LATE = 0, 1


def nt(left, right):
    return lax.dot_general(
        left, right, (((1,), (1,)), ((), ())), preferred_element_type=F32
    )


def nn(left, right):
    return jnp.dot(left, right, preferred_element_type=F32)


def kernel(
    master_in, grad_out_in, pre_mid_in, pre_up_in, coarse_in,
    coarse_grad, summed,
    master, grad_out, pre_mid, pre_up, coarse,
    g0, g1, g2, sb0, sb1, sb2, rb0, rb1, rb2, t0, t1, t2, ra0, ra1, ra2,
    u0, u1, u2, rc0, rc1, rc2, v0, v1, v2, rd0, rd1, rd2,
    wflat, fflat, w_one, w_two, w_up, x_out, x_mid, act_mid, act_up, mid_raw, up_raw, up_before,
    gathered, lowest, halo_out, halo_mid, halo_up,
    ag_send, ag_recv, core_send, core_recv, rs_send, rs_recv, swap_send, swap_recv,
    halo_send, halo_recv, load_sem, token_sem,
):
    gat, sbs, rbs, tot = (g0, g1, g2), (sb0, sb1, sb2), (rb0, rb1, rb2), (t0, t1, t2)
    ras, us, rcs, vs, rds = (
        (ra0, ra1, ra2), (u0, u1, u2), (rc0, rc1, rc2), (v0, v1, v2), (rd0, rd1, rd2),
    )
    slab, dp = lax.axis_index("slab"), lax.axis_index("dp")
    at = {
        "x": lax.rem(slab // 4, 4),
        "y": (slab // 16) * 2 + dp // 2,
        "z": lax.rem(slab, 4),
    }
    core = lax.rem(dp, 2)
    other = 1 - core

    def device(where, which):
        return (
            (where["y"] // 2) * 16 + where["x"] * 4 + where["z"],
            lax.rem(where["y"], 2) * 2 + which,
        )

    def moved(axis, step):
        where = dict(at)
        where[axis] = lax.rem(at[axis] + step, 4)
        return where

    def ahead(axis, step):
        return device(moved(axis, step), core)

    partner = device(at, other)
    after = (lax.rem(slab + 1, 32), dp)
    before = (lax.rem(slab + 31, 32), dp)

    def copy(src, dst, send, recv, target):
        return pltpu.make_async_remote_copy(
            src_ref=src, dst_ref=dst, send_sem=send, recv_sem=recv,
            device_id=target, device_id_type=MESH,
        )

    barrier = pltpu.get_barrier_semaphore()
    targets = [partner]
    targets += [ahead(axis, step) for axis in ("x", "y", "z") for step in (1, 2, 3)]
    for target in targets:
        pl.semaphore_signal(barrier, inc=1, device_id=target, device_id_type=MESH)

    def block(ref, part, lead, where):
        axes = ORDER[part]
        if part == 2:
            inner = [lax.rem(where["y"], 2), where["x"], where["z"]]
        else:
            inner = [where[axes[2]], where[axes[1]], lax.rem(where["y"], 2)]
        return tuple([where["y"] // 2] + lead + inner)

    loads = [
        pltpu.make_async_copy(src, dst, load_sem.at[number])
        for number, (src, dst) in enumerate(
            (
                (master_in, master),
                (grad_out_in, grad_out),
                (pre_mid_in, pre_mid),
                (pre_up_in, pre_up),
                (coarse_in, coarse.at[0, :, 0:2]),
            )
        )
    ]
    for load in loads:
        load.start()

    loads[0].wait()
    for part in range(3):
        rows = master[START[part] : START[part] + VALID[part], :]
        if HOLD[part] > VALID[part]:
            rows = jnp.concatenate(
                [rows, jnp.zeros((HOLD[part] - VALID[part], 128), F32)], axis=0
            )
        gat[part][block(gat[part], part, [core], at)] = rows.astype(BF16)
    pl.semaphore_wait(barrier, len(targets))

    started = []

    def go(c):
        c.start()
        started.append(c)
        return c

    def piece(part, which, level, half, where):
        place = block(gat[part], part, [which], where)
        if part == 2:
            return gat[part].at[place[: 5 - level]]
        if level == 0:
            return gat[part].at[place]
        return gat[part].at[(half,) + place[1 : 5 - level]]

    def back_half(step):
        return lax.rem(at["y"] + 4 - step, 4) // 2

    def gather(part, level, half):
        axis = ORDER[part][level]
        out = []
        for step in (1, 3, 2):
            sem = (part, level, step - 1, half)
            src = piece(part, core, level, half, at)
            go(copy(src, src, ag_send.at[sem], ag_recv.at[sem], ahead(axis, step)))
            dst = piece(part, core, level, half, moved(axis, 4 - step))
            out.append(copy(dst, dst, ag_send.at[sem], ag_recv.at[sem], partner))
        return out

    tall_half = at["y"] // 2
    tall = []
    for step in (1, 3, 2):
        sem = (2, 2, step - 1, 0)
        src = piece(2, core, 2, 0, at)
        dst = piece(2, core, 2, 0, moved("y", 4 - step))
        tall.append(
            (
                step,
                back_half(step),
                copy(src, src, ag_send.at[sem], ag_recv.at[sem], ahead("y", step)),
                copy(dst, dst, ag_send.at[sem], ag_recv.at[sem], partner),
            )
        )

    def tall_start(half):
        for _, _, c, _ in tall:
            pl.when(tall_half == half)(c.start)

    def tall_forward(half):
        for step, owner, _, c in tall:

            @pl.when(owner == half)
            def _():
                c.wait_recv()
                core_copy(2, 0, step, core).start()

    def tall_partner(half):
        for step, owner, _, _ in tall:
            pl.when(owner == half)(core_copy(2, 0, step, other).wait_recv)

    def core_copy(part, half, number, which):
        axis = ORDER[part][2]
        ref = piece(part, which, 2, half, moved(axis, 4 - number))
        sem = (part, half, number)
        return copy(ref, ref, core_send.at[sem], core_recv.at[sem], partner)

    def wait_for(copies):
        for c in copies:
            c.wait_recv()

    leg = [gather(part, 0, EARLY) for part in range(3)]
    for step in (1, 3, 2):
        pl.semaphore_signal(token_sem.at[0], inc=1, device_id=ahead("z", step), device_id_type=MESH)

    row = lax.broadcasted_iota(jnp.int32, (128, 128), 0)
    lane = lax.broadcasted_iota(jnp.int32, (128, 128), 1)
    breadth = lax.rem(row, 16)
    for ext in (x_out, x_mid):
        ext[:, :, 0] = jnp.zeros((2, 6, 16, 384), BF16)
        ext[:, :, 9] = jnp.zeros((2, 6, 16, 384), BF16)
    fflat[TOTAL : TOTAL + 8, :] = jnp.zeros((8, 128), F32)

    def widen(ext, sample, layer, value):
        later = jnp.where(breadth == 15, 0.0, pltpu.roll(value, 127, 0))
        earlier = jnp.where(breadth == 0, 0.0, pltpu.roll(value, 1, 0))
        wide = jnp.concatenate(
            [later.astype(BF16), value.astype(BF16), earlier.astype(BF16)], axis=1
        )
        ext[sample, layer, 1:9] = wide.reshape(8, 16, 384)

    def turn(act_t, first, value):
        turned = jnp.maximum(value, 0.0).T
        columns = slice(first * 128, first * 128 + 128)
        low = jnp.where(lane < 16, 0.0, pltpu.roll(turned, 16, 1))
        high = jnp.where(lane >= 112, 0.0, pltpu.roll(turned, 112, 1))
        act_t[0:128, columns] = low.astype(BF16)
        act_t[128:256, columns] = turned.astype(BF16)
        act_t[256:384, columns] = high.astype(BF16)

    def transposed_act(act_t, pre, depth, first):
        for sample in range(2):
            for layer in range(4):
                value = pre[sample, layer].reshape(128, 128).astype(F32)
                turn(act_t, sample * depth + first + layer, value)

    def transposed_edges(act_t, halo):
        for sample in range(2):
            low = halo[0, sample].reshape(128, 128).astype(F32)
            turn(act_t, sample * 6, jnp.where(slab > 0, low, 0.0))
            high = halo[1, sample].reshape(128, 128).astype(F32)
            turn(act_t, sample * 6 + 5, jnp.where(slab < 31, high, 0.0))

    def own_layers(index, carry):
        sample, layer = index // 4, lax.rem(index, 4)
        widen(x_out, sample, layer + 1, grad_out[sample, layer].reshape(128, 128).astype(F32))
        return carry

    def edges(ext, halo):
        for sample in range(2):
            low = halo[0, sample].reshape(128, 128).astype(F32)
            widen(ext, sample, 0, jnp.where(slab > 0, low, 0.0))
            high = halo[1, sample].reshape(128, 128).astype(F32)
            widen(ext, sample, 5, jnp.where(slab < 31, high, 0.0))

    def grad_by_cotangent(ext, act_t, first, depth):
        right = ext[:, 2 - depth : 6 - depth, 1:9].reshape(1024, 384)
        store_grad(first, depth, nn(act_t[...], right))

    def grad_by_act(ext, act_t, first, depth):
        out = jnp.zeros((384, 384), F32)
        for sample in range(2):
            start = (sample * 6 + depth) * 128
            out = out + nn(act_t[:, start : start + 512], ext[sample, 1:5, 1:9].reshape(512, 384))
        store_grad(first, depth, out)

    def store_grad(first, depth, out):
        for height in range(3):
            for col in range(3):
                start = first + ((depth * 3 + height) * 3 + col) * 128
                fflat[start : start + 128, :] = out[
                    height * 128 : height * 128 + 128, col * 128 : col * 128 + 128
                ]

    def back_conv(ext, weight, layers):
        acc = jnp.zeros((512, 128), F32)
        for depth in range(3):
            for height in range(3):
                rows = slice(2 - height, 10 - height)
                left = jnp.concatenate(
                    [ext[:, layer + 2 - depth, rows].reshape(256, 384) for layer in layers], axis=0
                )
                acc = acc + nt(left, weight[depth * 3 + height])
        return acc

    def place(chip):
        return {"x": lax.rem(chip // 8, 4), "y": (chip // 32) * 2 + lax.rem(chip, 2), "z": lax.rem(chip // 2, 4)}

    def unpack(chip, carry):
        where = place(chip)
        base = pl.multiple_of(chip * 216, 8)
        pieces = []
        for which in range(2):
            for part in range(3):
                value = gat[part][block(gat[part], part, [which], where)]
                pieces.append(value.astype(F32)[: VALID[part]])
        wflat[pl.ds(base, 216), :] = jnp.concatenate(pieces, axis=0)
        return carry

    def taps(weight, first, width):
        def one(index, carry):
            for col in range(3):
                start = pl.multiple_of((index * 3 + col) * width + first, 128)
                weight[index, :, col * 128 : col * 128 + 128] = wflat[pl.ds(start, width), :].astype(BF16)
            return carry

        lax.fori_loop(0, 9, one, 0)

    def pack(chip, carry):
        where = place(chip)
        base = pl.multiple_of(chip * 216, 8)
        value = fflat[pl.ds(base, 224), :]
        for which in range(2):
            for part in range(3):
                start = which * ROWS + START[part]
                rows = value[start : start + HOLD[part]].astype(BF16)
                sbs[part][block(sbs[part], part, [which], where)[1:]] = rows
        return carry

    def pack_late(chip, carry):
        where = place(chip)
        base = pl.multiple_of(chip * 216, 8)
        value = fflat[pl.ds(base, 224), :]
        value = jnp.where(core == 0, value[0:112], value[ROWS : ROWS + 112])
        for part in range(3):
            rows = value[START[part] : START[part] + HOLD[part]].astype(BF16)
            tot[part][block(tot[part], part, [], where)] = rows
        return carry

    def swap(first):
        out = []
        for part in range(3):
            group = pl.ds(first, 2)
            if part == 0:
                src, dst = sbs[0].at[other, group], rbs[0].at[group]
            else:
                src, dst = sbs[part].at[other, :, group], rbs[part].at[:, group]
            sem = (part, first // 2)
            out.append(go(copy(src, dst, swap_send.at[sem], swap_recv.at[sem], partner)))
        return out

    def core_sums(first, swapped):
        for part in range(3):
            swapped[part].wait_recv()

            def add(index, carry, part=part):
                if part == 0:
                    a, b = first + index // 4, lax.rem(index, 4)
                else:
                    a, b = index // 2, first + lax.rem(index, 2)
                total = sbs[part][core, a, b].astype(F32) + rbs[part][a, b].astype(F32)
                tot[part][EARLY, a, b] = total.astype(BF16)
                return carry

            lax.fori_loop(0, (8, 8, 4)[part], add, 0)

    def scatter(part, level, src, dst, sems):
        axis = ORDER[part][2 - level]
        out = []
        for step in (1, 3, 2):
            sem = (part, level, step - 1, sems)
            out.append(
                go(
                    copy(
                        src.at[lax.rem(at[axis] + step, 4)], dst.at[step - 1],
                        rs_send.at[sem], rs_recv.at[sem], ahead(axis, step),
                    )
                )
            )
        return out

    early_x, early_z, column = [], [], []
    for step in (1, 3, 2):
        where = moved("x", step)
        sem = (0, 0, step - 1, 0)
        c = copy(
            tot[0].at[EARLY, where["x"]], ras[0].at[EARLY, step - 1],
            rs_send.at[sem], rs_recv.at[sem], device(where, core),
        )
        early_x.append((where["x"] // 2 * 2, c))
        where = moved("y", step)
        owner = where["y"] // 2
        for number, group in enumerate((pl.ds(2, 2), pl.ds(0, 2), pl.ds(0, 4))):
            sem = (2, 0, step - 1, number)
            c = copy(
                tot[2].at[where["y"] // 2, lax.rem(where["y"], 2), group],
                ras[2].at[step - 1, group],
                rs_send.at[sem], rs_recv.at[sem], device(where, core),
            )
            column.append((number, owner, c))

    def early_sends(first):
        number = 1 - first // 2
        for owner, c in early_x:
            pl.when(owner == first)(c.start)
        group = pl.ds(first, 2)
        for step in (1, 3, 2):
            where = moved("z", step)
            sem = (1, 0, step - 1, number)
            early_z.append(
                go(
                    copy(
                        tot[1].at[EARLY, where["z"], group], ras[1].at[EARLY, step - 1, group],
                        rs_send.at[sem], rs_recv.at[sem], device(where, core),
                    )
                )
            )
        for which, owner, c in column:
            if which == number:
                pl.when(owner == EARLY)(c.start)

    def late_sends():
        for which, owner, c in column:
            if which == 2:
                pl.when(owner == LATE)(c.start)
        return [scatter(part, 0, tot[part].at[LATE], ras[part].at[LATE], 2) for part in range(2)]

    for load in loads[1:]:
        load.wait()
    transposed_act(act_mid, pre_mid, 4, 0)
    for part in range(3):
        wait_for(leg[part])
    leg = [gather(part, 1, EARLY) for part in range(3)]
    pl.semaphore_wait(token_sem.at[0], 3)
    pl.semaphore_signal(token_sem.at[1], inc=1, device_id=ahead("y", 2), device_id_type=MESH)
    lax.fori_loop(0, 8, own_layers, 0)
    grad_by_cotangent(x_out, act_mid, FILTER, 1)
    pl.semaphore_wait(token_sem.at[1], 1)
    halos = []
    for number, (src, dst, target) in enumerate(
        (
            (grad_out.at[:, 3], halo_out.at[0], after),
            (grad_out.at[:, 0], halo_out.at[1], before),
            (pre_up.at[:, 3], halo_up.at[0], after),
            (pre_up.at[:, 0], halo_up.at[1], before),
            (coarse.at[0, :, 0], coarse.at[0, :, 2], before),
        )
    ):
        sem = 3 + number
        halos.append(go(copy(src, dst, halo_send.at[sem], halo_recv.at[sem], target)))
    third = []
    for part in (2, 0, 1):
        wait_for(leg[part])
        if part == 2:
            tall_start(EARLY)
        else:
            third.append(gather(part, 2, EARLY))
        go(core_copy(part, EARLY, 0, core))
    leg = [gather(part, 1, LATE) for part in range(2)]
    transposed_act(act_up, pre_up, 6, 1)
    wait_for(halos[0:2])
    edges(x_out, halo_out)
    grad_by_cotangent(x_out, act_mid, FILTER, 0)
    grad_by_cotangent(x_out, act_mid, FILTER, 2)
    lax.fori_loop(16, 32, pack, 0)
    two_swap = swap(2)

    def forward(part, half, copies):
        for step, c in zip((1, 3, 2), copies):
            c.wait_recv()
            go(core_copy(part, half, step, core))

    tall_forward(EARLY)
    for part in range(2):
        forward(part, EARLY, third[part])
    third = []
    for part in range(2):
        wait_for(leg[part])
        third.append(gather(part, 2, LATE))
        go(core_copy(part, LATE, 0, core))
    tall_start(LATE)
    wait_for(halos[2:])
    pair = go(copy(coarse.at[0], coarse.at[1], halo_send.at[8], halo_recv.at[8], partner))
    transposed_edges(act_up, halo_up)
    core_copy(2, EARLY, 0, other).wait_recv()
    tall_partner(EARLY)
    for part in range(2):
        wait_for([core_copy(part, EARLY, number, other) for number in range(4)])

    lax.fori_loop(16, 32, unpack, 0)
    taps(w_two, FILTER, 128)

    def mid_layers(layers):
        both = back_conv(x_out, w_two, layers)
        for number, layer in enumerate(layers):
            value = both[number * 256 : number * 256 + 256]
            keep = pre_mid[:, layer].reshape(256, 128).astype(F32) > 0.0
            value = jnp.where(keep, value, 0.0).astype(BF16)
            mid_raw[:, layer] = value.reshape(2, 8, 16, 128)

    def widen_mid(layers):
        for layer in layers:
            for sample in range(2):
                widen(x_mid, sample, layer + 1, mid_raw[sample, layer].reshape(128, 128).astype(F32))

    mid_layers((3, 0))
    mid_up = go(copy(mid_raw.at[:, 3], halo_mid.at[0], halo_send.at[0], halo_recv.at[0], after))
    mid_down = go(copy(mid_raw.at[:, 0], halo_mid.at[1], halo_send.at[1], halo_recv.at[1], before))
    core_sums(2, two_swap)
    early_sends(2)
    mid_layers((1, 2))
    widen_mid((0, 1, 2, 3))
    for depth in range(3):
        grad_by_act(x_mid, act_up, 0, depth)
    lax.fori_loop(0, 16, pack, 0)
    one_swap = swap(0)
    lax.fori_loop(0, 16, unpack, 0)
    taps(w_one, 0, 128)
    core_sums(0, one_swap)
    early_sends(0)
    tall_forward(LATE)
    for part in range(2):
        forward(part, LATE, third[part])
    pair.wait_recv()
    turned = []
    for first in (1, 0):
        rows = []
        for slot in range(2):
            for sample in range(2):
                for quarter in (first, first + 1):
                    value = coarse[slot, sample, quarter].astype(F32)
                    if quarter == 2:
                        value = jnp.where(slab < 31, value, 0.0)
                    rows.append(value)
        turned.append(jnp.concatenate(rows, axis=0).T.astype(BF16))
    mid_up.wait_recv()
    mid_down.wait_recv()
    edges(x_mid, halo_mid)

    up_pair = []
    for layers in ((3, 0), (1, 2)):
        both = back_conv(x_mid, w_one, layers)
        for number, layer in enumerate(layers):
            value = both[number * 256 : number * 256 + 256]
            keep = pre_up[:, layer].reshape(256, 128).astype(F32) > 0.0
            value = jnp.where(keep, value, 0.0).astype(BF16)
            up_raw[0, :, layer] = value.reshape(2, 128, 128)
        if layers[0] == 3:
            up_next = go(copy(up_raw.at[0, :, 3], up_before, halo_send.at[9], halo_recv.at[9], after))
            cuts = ((2, slice(3, 4)), (10, slice(0, 1)))
        else:
            cuts = ((11, slice(1, 3)),)
        for sem, cut in cuts:
            src, dst = up_raw.at[0, :, cut], up_raw.at[1, :, cut]
            up_pair.append(go(copy(src, dst, halo_send.at[sem], halo_recv.at[sem], partner)))

    def second_sums(part, half, copies):
        wait_for(copies)
        mine = at[ORDER[part][2]]

        def add(index, carry):
            total = tot[part][half, mine, index].astype(F32)
            for step in range(3):
                total = total + ras[part][half, step, index].astype(F32)
            us[part][half, index] = total.astype(BF16)
            return carry

        lax.fori_loop(0, 4, add, 0)
        return scatter(part, 1, us[part].at[half], rcs[part].at[half], half)

    def third_sums(part, half, copies):
        wait_for(copies)
        total = us[part][half, at[ORDER[part][1]]].astype(F32)
        for step in range(3):
            total = total + rcs[part][half, step].astype(F32)
        vs[part][2 * half : 2 * half + 2] = total.astype(BF16)

    pick_row = lax.broadcasted_iota(jnp.int32, (288, 128), 0)
    pick_lane = lax.broadcasted_iota(jnp.int32, (288, 128), 1)
    tap, coarse_row, coarse_col = pick_row // 32, lax.rem(pick_row // 8, 4), lax.rem(pick_row, 8)
    fine_row = 2 * coarse_row + tap // 3 - 1
    fine_col = 2 * coarse_col + lax.rem(tap, 3) - 1
    chosen = (fine_row >= 0) & (fine_col >= 0) & (pick_lane == fine_row * 16 + fine_col)
    pick = jnp.where(chosen, 1.0, 0.0).astype(BF16)

    def spread(slot, sample, layer):
        picked = nn(pick, up_raw[slot, sample, layer]).astype(BF16)
        first = ((slot * 2 + sample) * 2 + layer // 2) * 32
        for depth in (1,) if layer % 2 == 0 else (0, 2):
            for tap in range(9):
                columns = slice((depth * 9 + tap) * 128, (depth * 9 + tap) * 128 + 128)
                gathered[first : first + 32, columns] = picked[tap * 32 : tap * 32 + 32]
        return picked

    def lower(sample, quarter, picked):
        first = (sample * 2 + quarter) * 32
        for tap in range(9):
            lowest[first : first + 32, tap * 128 : tap * 128 + 128] = picked[tap * 32 : tap * 32 + 32]

    for sample in range(2):
        for layer in range(4):
            picked = spread(0, sample, layer)
            if layer == 1:
                lower(sample, 1, picked)
    wait_for(up_pair)
    for sample in range(2):
        for layer in range(4):
            spread(1, sample, layer)
    for index in range(9):
        out = nn(turned[min(index // 3, 1)], gathered[:, index * 384 : index * 384 + 384])
        for col in range(3):
            start = 2 * FILTER + (index * 3 + col) * 256
            fflat[start : start + 256, :] = out[:, col * 128 : col * 128 + 128]
    lax.fori_loop(32, 64, pack_late, 0)
    late_first = late_sends()
    early_first = ([c for _, c in early_x], early_z)

    tall_partner(LATE)
    for part in range(2):
        wait_for([core_copy(part, LATE, number, other) for number in range(4)])
    lax.fori_loop(32, 64, unpack, 0)
    taps(w_up, 2 * FILTER, 256)
    up_next.wait_recv()
    for sample in range(2):
        value = jnp.where(slab > 0, up_before[sample].astype(F32), 0.0).astype(BF16)
        lower(sample, 0, nn(pick, value).astype(BF16))
    acc = jnp.zeros((128, 256), F32)
    for index in range(9):
        if index < 3:
            left = lowest[:, index * 384 : index * 384 + 384]
        else:
            left = gathered[0:128, index * 384 : index * 384 + 384]
        acc = acc + nt(left, w_up[index])
    coarse_grad[...] = acc.astype(BF16)
    early_second = [second_sums(part, EARLY, early_first[part]) for part in range(2)]

    for which, _, c in column:
        pl.when(tall_half == (LATE if which == 2 else EARLY))(c.wait_recv)
    mine = (at["y"] // 2, lax.rem(at["y"], 2))

    def add_plane(index, carry):
        total = tot[2][mine[0], mine[1], index].astype(F32)
        for step in range(3):
            total = total + ras[2][step, index].astype(F32)
        us[2][index] = total.astype(BF16)
        return carry

    lax.fori_loop(0, 4, add_plane, 0)
    plane = scatter(2, 1, us[2], rcs[2], 0)
    late_second = [second_sums(part, LATE, late_first[part]) for part in range(2)]
    for part in range(2):
        third_sums(part, EARLY, early_second[part])
    wait_for(plane)
    total = us[2][at["x"]].astype(F32)
    for step in range(3):
        total = total + rcs[2][step].astype(F32)
    vs[2][...] = total.astype(BF16)
    last = [None, None, scatter(2, 2, vs[2], rds[2], 0)]
    for part in range(2):
        third_sums(part, LATE, late_second[part])
        last[part] = scatter(part, 2, vs[part], rds[part], 0)
    for part in (2, 0, 1):
        wait_for(last[part])
        total = vs[part][at[ORDER[part][0]]].astype(F32)
        for step in range(3):
            total = total + rds[part][step].astype(F32)
        summed[START[part] : START[part] + VALID[part], :] = total[: VALID[part]]
    for c in started:
        c.wait_send()
    for _, c in early_x:
        c.wait_send()
    for which, owner, c in column:
        pl.when(owner == (LATE if which == 2 else EARLY))(c.wait_send)
    for step, _, c, _ in tall:
        c.wait_send()
        core_copy(2, 0, step, core).wait_send()


def finish(coarse, summed, master, moment, second, coarse_grad, new_master, new_moment, new_second):
    coarse_grad[...] = coarse[...].astype(F32).reshape(coarse_grad.shape).astype(BF16)
    mean_grad = summed[...] / 8.0
    first = beta_one * moment[...] + (1.0 - beta_one) * mean_grad
    squared = beta_two * second[...] + (1.0 - beta_two) * mean_grad * mean_grad
    corrected = first / (1.0 - beta_one**adam_step)
    scaled = jnp.sqrt(squared / (1.0 - beta_two**adam_step)) + adam_eps
    new_moment[...] = first
    new_second[...] = squared
    new_master[...] = master[...] - learn_rate * corrected / scaled


def body(coarse_in, pre_up, pre_mid, grad_out, master, moment, second):
    vmem = pl.BlockSpec(memory_space=pltpu.VMEM)
    held = pl.BlockSpec(memory_space=pl.ANY)
    scratch = [
        pltpu.VMEM((ROWS, 128), F32),
        pltpu.VMEM((2, 4, 8, 16, 128), BF16),
        pltpu.VMEM((2, 4, 8, 16, 128), BF16),
        pltpu.VMEM((2, 4, 8, 16, 128), BF16),
        pltpu.VMEM((2, 2, 3, 32, 256), BF16),
    ]
    for shape, column in (
        ((2, 2, 4, 4, 2), (2, 2, 2, 4, 4)),
        ((2, 4, 4, 2), (2, 2, 4, 4)),
        ((4, 4, 2), (2, 4, 4)),
        ((2, 4, 4, 2), (2, 2, 4, 4)),
        ((2, 3, 4, 2), (3, 4, 4)),
        ((2, 4, 2), (4, 4)),
        ((2, 3, 2), (3, 4)),
        ((4,), (4,)),
        ((3,), (3,)),
    ):
        for part in range(3):
            lead = column if part == 2 else shape
            scratch.append(pltpu.VMEM(lead + (HOLD[part], 128), BF16))
    scratch += [
        pltpu.VMEM((TOTAL, 128), F32),
        pltpu.VMEM((TOTAL + 8, 128), F32),
        pltpu.VMEM((9, 128, 384), BF16),
        pltpu.VMEM((9, 128, 384), BF16),
        pltpu.VMEM((9, 256, 384), BF16),
        pltpu.VMEM((2, 6, 10, 16, 384), BF16),
        pltpu.VMEM((2, 6, 10, 16, 384), BF16),
        pltpu.VMEM((384, 1024), BF16),
        pltpu.VMEM((384, 1536), BF16),
        pltpu.VMEM((2, 4, 8, 16, 128), BF16),
        pltpu.VMEM((2, 2, 4, 128, 128), BF16),
        pltpu.VMEM((2, 128, 128), BF16),
        pltpu.VMEM((256, FILTER), BF16),
        pltpu.VMEM((128, 9 * 128), BF16),
        pltpu.VMEM((2, 2, 8, 16, 128), BF16),
        pltpu.VMEM((2, 2, 8, 16, 128), BF16),
        pltpu.VMEM((2, 2, 8, 16, 128), BF16),
    ]
    for shape in ((3, 3, 3, 2), (3, 2, 4), (3, 3, 3, 3), (3, 2), (12,)):
        scratch += [pltpu.SemaphoreType.DMA(shape)] * 2
    scratch += [pltpu.SemaphoreType.DMA((5,)), pltpu.SemaphoreType.REGULAR((2,))]
    coarse_grad, summed = pl.pallas_call(
        kernel,
        out_shape=(
            jax.ShapeDtypeStruct((128, 256), BF16),
            jax.ShapeDtypeStruct((ROWS, 128), F32),
        ),
        in_specs=[held] * 5,
        out_specs=(vmem, vmem),
        scratch_shapes=scratch,
        compiler_params=pltpu.CompilerParams(
            collective_id=0, has_side_effects=True, vmem_limit_bytes=56 * 1024 * 1024
        ),
    )(
        master,
        grad_out.reshape(grad_out.shape[1:]),
        pre_mid.reshape(pre_mid.shape[1:]),
        pre_up.reshape(pre_up.shape[1:]),
        coarse_in.reshape(2, 2, 32, 256),
    )
    coarse_shape = jax.ShapeDtypeStruct(coarse_in.shape, BF16)
    rows_shape = jax.ShapeDtypeStruct((ROWS, 128), F32)
    return tuple(
        pl.pallas_call(
            finish,
            out_shape=(coarse_shape, rows_shape, rows_shape, rows_shape),
            in_specs=[vmem] * 5,
            out_specs=(vmem,) * 4,
        )(coarse_grad, summed, master, moment, second)
    )


def solution(mesh):
    wide = P("dp", None, "slab", None, None, None)
    flat = P(("slab", "dp"), None)
    return jax.shard_map(
        body,
        mesh=mesh,
        in_specs=(wide, wide, wide, wide, flat, flat, flat),
        out_specs=(wide, flat, flat, flat),
        check_vma=False,
    )
```
